32 devices in a mesh: dp: 8 (over y, x, core), phase: 4 (over z).
Axes of the slice: x: 2, y: 2, z: 4, core: 2. Of those that a mesh axis runs over, the one named last changes fastest.
Arguments:
- patches: bfloat16 [4096, 1280], P(('dp', 'phase')), may hold values from -6 to 6
- window_ids: int32 [32, 128], P(('dp', 'phase')), may hold values from 0 to 3, never falling along the last dimension, each value on 1 to 64 neighbouring positions
- norm_gain: float32 [4, 1280], replicated, may hold values from 0.1 to 1.9
- w_qkv: bfloat16 [4, 1280, 1920], P(None, 'dp')
- w_out: bfloat16 [4, 640, 1280], P(None, 'dp'), may hold values from -0.25 to 0.25
- merge_gain: float32 [1280], replicated, may hold values from 0.1 to 1.9
Outputs:
- merged: bfloat16 [1024, 5120], P(('dp', 'phase'))
The draws below stay inside these ranges and needn't reach their ends.
Inputs may be any that keep to these rules, and one draw needn't show every extreme that they name: `window_ids`: window numbers never fall along a micro-batch; each window holds 1 to 64 patches, one exactly 64.
All inputs are finite; a program needn't handle non-finite values.
Results may differ from the reference program's by a relative error of at most 0.028.
Values may be sent and summed in bfloat16 or wider, within the bound.
No kernel may reach another device: no remote copies, remote signals or barrier semaphores. Data moves between devices by JAX's collectives and lax.ppermute only.
A program may use at most 64 MiB of HBM per device.

```python
import math
import jax
import jax.numpy as jnp
import numpy as np
from jax import lax

D_VIS = 1280
HEADS = 8
HEAD_DIM = 80
MB = 128
SECTIONS = 4
WIN_MOST = 64
WINDOWS = 4
MICRO = 32


def draw_w_qkv(key, part):
    width = HEADS * HEAD_DIM
    base = jax.random.normal(key, (SECTIONS, D_VIS, 3 * width), jnp.float32) * D_VIS ** (-0.5)
    return base.astype(jnp.bfloat16)


def block_levels(stream_key, shape, shards, low, high):
    loudness, own = 1.0, jax.random.fold_in(stream_key, 6)
    for axis_at, blocks in shards:
        steps = jnp.exp(jax.random.uniform(jax.random.fold_in(own, axis_at), (blocks,), jnp.float32, low / len(shards), high / len(shards)))
        loudness = loudness * jnp.repeat(steps, shape[axis_at] // blocks).reshape([-1 if axis == axis_at else 1 for axis in range(len(shape))])
    return loudness


def length_profile(amount, total, reach, lean):
    loads = [(1 << 20) // math.isqrt(rank ** lean) + 1 for rank in range(2, amount + 1)]
    rest, given = total - reach - (amount - 1), [1] * (amount - 1)
    while rest > 0:
        movable = [i for i in range(amount - 1) if given[i] < reach]
        whole, remaining = sum([loads[i] for i in movable]), rest
        for i in movable:
            more = min(reach - given[i], max(1, remaining * loads[i] // whole), rest)
            given[i] = given[i] + more
            rest = rest - more
    return np.array([reach] + given)


def uneven(stream_key, count, total, limit, slope):
    if count == 2:
        one = jax.random.randint(stream_key, (), max(1, total - limit), min(limit, total - 1) + 1)
        return jnp.stack([one, total - one])
    lengths = jnp.asarray(length_profile(count, total, limit, slope), jnp.int32)
    twos = (count - 1) // 2
    donor, sink = lengths[1:1 + 2 * twos:2], lengths[2:2 + 2 * twos:2]
    margin = jnp.minimum(donor - 1, limit - sink)
    passed = jax.random.randint(jax.random.fold_in(stream_key, 1), (twos,), 0, 1 << 20) % (margin + 1)
    lengths = lengths.at[1:1 + 2 * twos:2].set(donor - passed).at[2:2 + 2 * twos:2].set(sink + passed)
    return lengths[jax.random.permutation(jax.random.fold_in(stream_key, 2), count)]


def gaussian(stream_key, dims, scale, bound, pieces=(), kind=jnp.bfloat16):
    result = jax.random.normal(stream_key, dims, jnp.float32) * scale
    if len(pieces) > 0:
        result = block_levels(stream_key, dims, pieces, -0.22, 0.18) * result
    return jnp.clip(result, min=-bound, max=bound).astype(kind)


def setup_inputs(seed: int = 0) -> dict:
    splits = jax.random.split(jax.random.key(seed), 7)
    patches = gaussian(splits[0], (MICRO * MB, D_VIS), 1.0, 6.0, ((0, 32),))
    window_ids = jax.vmap(lambda own: jnp.searchsorted(jnp.cumsum(uneven(own, WINDOWS, MB, WIN_MOST, 1)), jnp.arange(MB), side="right"))(jax.random.split(splits[1], MICRO)).reshape((MICRO, MB)).astype(jnp.int32)
    norm_gain = jnp.clip(1.0 + 0.18 * jax.random.normal(splits[2], (SECTIONS, D_VIS), jnp.float32), 0.1, 1.9)
    w_qkv = draw_w_qkv(jax.random.fold_in(splits[6], 71), 0)
    w_out = gaussian(splits[4], (SECTIONS, HEADS * HEAD_DIM, D_VIS), (HEADS * HEAD_DIM) ** -0.5, 0.25, ((1, 8),))
    merge_gain = jnp.clip(1.0 + 0.18 * jax.random.normal(splits[5], (D_VIS,), jnp.float32), 0.1, 1.9)
    return {"patches": patches, "window_ids": window_ids, "norm_gain": norm_gain, "w_qkv": w_qkv, "w_out": w_out, "merge_gain": merge_gain}


def rms_scale(values, gain):
    return values * lax.rsqrt(lax.optimization_barrier(jnp.mean(values * values, axis=-1, keepdims=True)) + 1e-06) * gain

def section(acts, window_ids, gain, weight_qkv, weight_out):
    width = HEADS * HEAD_DIM
    batch = acts.shape[0]
    values_f = acts.astype(jnp.float32)
    normed = rms_scale(values_f, gain).astype(jnp.bfloat16)
    qkv = jnp.einsum('bmd,de->bme', normed.astype(jnp.float32), weight_qkv.astype(jnp.float32)).astype(jnp.bfloat16)
    query = qkv[..., :width].reshape(batch, MB, HEADS, HEAD_DIM).astype(jnp.float32)
    keys = qkv[..., width:2 * width].reshape(batch, MB, HEADS, HEAD_DIM).astype(jnp.float32)
    vals = qkv[..., 2 * width:].reshape(batch, MB, HEADS, HEAD_DIM).astype(jnp.float32)
    scores = jnp.einsum('bqhd,bkhd->bhqk', query, keys) * HEAD_DIM ** (-0.5)
    same = window_ids[:, :, None] == window_ids[:, None, :]
    scores = jnp.where(same[:, None], scores, jnp.float32(-1e+30))
    highest = lax.optimization_barrier(jnp.max(scores, axis=-1, keepdims=True))
    weights = jnp.exp(scores - highest)
    probs = (weights / lax.optimization_barrier(jnp.sum(weights, axis=-1, keepdims=True))).astype(jnp.bfloat16)
    context = jnp.einsum('bhqk,bkhd->bqhd', probs.astype(jnp.float32), vals).astype(jnp.bfloat16)
    context = context.reshape(batch, MB, width)
    update = jnp.einsum('bme,ed->bmd', context.astype(jnp.float32), weight_out.astype(jnp.float32))
    return (values_f + update).astype(jnp.bfloat16)

def reference(patches, window_ids, norm_gain, w_qkv, w_out, merge_gain):
    acts = patches.reshape(-1, MB, D_VIS)
    for index in range(SECTIONS):
        acts = section(acts, window_ids, norm_gain[index], w_qkv[index], w_out[index])
    final = rms_scale(acts.reshape(-1, D_VIS).astype(jnp.float32), merge_gain).astype(jnp.bfloat16)
    return final.reshape(-1, 4 * D_VIS)
```

```python
import functools

import jax
import jax.numpy as jnp
from jax import lax
from jax.experimental import pallas as pl
from jax.experimental.pallas import tpu as pltpu
from jax.sharding import PartitionSpec as P

D_VIS = 1280
HEADS = 8
HEAD_DIM = 80
WIDTH = HEADS * HEAD_DIM
SECTIONS = 4
LANES = 128
EPS = 1e-06
NEG = -1e30
BLOCKS = ((0, 0, 160), (2, 0, 160), (4, 0, 160), (6, 0, 80), (6, 80, 80),
          (1, 0, 160), (3, 0, 160), (5, 0, 160), (7, 0, 80), (7, 80, 80))


def normed_rows(values, gain):
    scale = lax.rsqrt(jnp.mean(values * values, axis=-1, keepdims=True) + EPS)
    return values * scale * gain


def attend(qkv, row_ids):
    query, keys, vals = qkv
    rows = query.shape[0]
    across = jnp.broadcast_to(row_ids, (rows, rows))
    same = across == across.T
    lane = lax.broadcasted_iota(jnp.int32, (rows, LANES), 1)
    tiles = [None] * (WIDTH // LANES)
    for head in range(HEADS):
        first, last = head * HEAD_DIM, (head + 1) * HEAD_DIM
        low, high = first // LANES, -(-last // LANES)
        span = slice(low * LANES, high * LANES)
        inside = []
        for tile in range(low, high):
            place = lane + tile * LANES
            inside.append((place >= first) & (place < last))
        part = jnp.concatenate(
            [
                jnp.where(mask, query[:, (low + i) * LANES : (low + i + 1) * LANES], 0)
                for i, mask in enumerate(inside)
            ],
            axis=1,
        )
        scores = lax.dot_general(
            part, keys[:, span], (((1,), (1,)), ((), ())), preferred_element_type=jnp.float32
        )
        scores = jnp.where(same, scores * HEAD_DIM ** (-0.5), NEG)
        weights = jnp.exp(scores - jnp.max(scores, axis=-1, keepdims=True))
        probs = weights * (1.0 / jnp.sum(weights, axis=-1, keepdims=True))
        mixed = jnp.dot(
            probs.astype(jnp.bfloat16), vals[:, span], preferred_element_type=jnp.float32
        )
        for i, mask in enumerate(inside):
            kept = jnp.where(mask, mixed[:, i * LANES : (i + 1) * LANES], 0.0)
            tile = low + i
            tiles[tile] = kept if tiles[tile] is None else tiles[tile] + kept
    return jnp.concatenate(tiles, axis=1).astype(jnp.bfloat16)


def stage_kernel(steps, loads, n_chunks, micros, acts_parts, with_ctx, with_acts, *refs):
    refs = list(refs)
    me_ref = refs.pop(0)
    acts_refs = [refs.pop(0) for _ in acts_parts]
    ctx_ref = refs.pop(0) if with_ctx else None
    ids_refs = [refs.pop(0) for _ in range(micros)]
    gain_ref = refs.pop(0)
    merge_ref = refs.pop(0)
    chunks = [[refs.pop(0) for _ in BLOCKS] for _ in range(n_chunks)]
    out_refs = refs[: with_acts]
    hold, flow, sheets, sems = refs[with_acts:]
    me = me_ref[0]
    for slot, (chunk, unit, is_out) in enumerate(loads):
        for (distance, start, size), block in zip(BLOCKS, chunks[chunk]):
            owner = jnp.bitwise_xor(me, distance)
            if not is_out:
                where = pl.multiple_of(owner * 160 + start, 16)
                pltpu.make_async_copy(
                    block.at[unit], hold.at[slot, pl.ds(where, size)], sems.at[slot]
                ).start()
            else:
                for half in range(start // 80, (start + size) // 80):
                    where = pl.multiple_of(owner * 80 + half * WIDTH, 16)
                    pltpu.make_async_copy(
                        block.at[unit, pl.ds(half * 80 - start, 80)],
                        hold.at[slot, pl.ds(where, 80)],
                        sems.at[slot],
                    ).start()

    def arrive(slot):
        pltpu.make_async_copy(hold.at[slot], hold.at[slot], sems.at[slot]).wait()

    rows = 128
    for m, (ref, row) in enumerate(zip(acts_refs, acts_parts)):
        flow[m * rows : (m + 1) * rows] = ref[row : row + rows].astype(jnp.float32)
    ctx = ctx_ref[...] if with_ctx else None
    for step in steps:
        if step[0] == "att":
            normed = normed_rows(flow[...], gain_ref[step[1]]).astype(jnp.bfloat16)
            qkv = []
            for i in range(3):
                arrive(step[2] + i)
                qkv.append(
                    jnp.dot(
                        normed, hold[step[2] + i], preferred_element_type=jnp.float32
                    ).astype(jnp.bfloat16)
                )
            parts = [
                attend([part[m * rows : (m + 1) * rows] for part in qkv], ids_refs[m][...])
                for m in range(micros)
            ]
            ctx = parts[0] if micros == 1 else jnp.concatenate(parts, axis=0)
        elif step[0] == "out":
            arrive(step[1])
            for half in range(2):
                at = slice(half * WIDTH, (half + 1) * WIDTH)
                moved = jnp.dot(
                    ctx, hold[step[1], half * WIDTH : (half + 1) * WIDTH],
                    preferred_element_type=jnp.float32,
                )
                flow[:, at] = (flow[:, at] + moved).astype(jnp.bfloat16).astype(jnp.float32)
        else:
            final = normed_rows(flow[...], merge_ref[...])
            for tile in range(D_VIS // LANES):
                sheets[tile] = final[:, tile * LANES : (tile + 1) * LANES]
    if steps[-1][0] == "att":
        out_refs[0][...] = ctx
    elif steps[-1][0] == "out":
        out_refs[0][...] = flow[...].astype(jnp.bfloat16)
    else:
        for i in range(4):
            for tile in range(D_VIS // LANES):
                at = i * D_VIS + tile * LANES
                out_refs[0][:, at : at + LANES] = sheets[
                    tile, pl.ds(i, rows // 4, stride=4), :
                ].astype(jnp.bfloat16)


def run_stage(name, steps, loads, me, acts, ctx, ids, gains, merge, chunks):
    micros = len(acts)
    rows = 128
    last = steps[-1][0]
    shape = {
        "att": (micros * rows, WIDTH),
        "out": (micros * rows, D_VIS),
        "norm": (rows // 4, 4 * D_VIS),
    }[last]
    kernel = functools.partial(
        stage_kernel, steps, loads, len(chunks), micros, [row for _, row in acts],
        ctx is not None, 1,
    )
    vmem = pl.BlockSpec(memory_space=pltpu.VMEM)
    args = [me] + [a for a, _ in acts] + ([ctx] if ctx is not None else []) + list(ids)
    args += [gains, merge]
    specs = [pl.BlockSpec(memory_space=pltpu.SMEM)] + [vmem] * (len(args) - 1)
    for chunk in chunks:
        args += list(chunk)
        specs += [pl.BlockSpec(memory_space=pl.ANY)] * len(chunk)
    units = len(loads)
    return pl.pallas_call(
        kernel,
        out_shape=jax.ShapeDtypeStruct(shape, jnp.bfloat16),
        in_specs=specs,
        out_specs=vmem,
        scratch_shapes=[
            pltpu.VMEM((units, D_VIS, WIDTH), jnp.bfloat16),
            pltpu.VMEM((micros * rows, D_VIS), jnp.float32),
            pltpu.VMEM((D_VIS // LANES, rows, LANES), jnp.float32),
            pltpu.SemaphoreType.DMA((units,)),
        ],
        compiler_params=pltpu.CompilerParams(vmem_limit_bytes=40 * 1024 * 1024),
        cost_estimate=pl.CostEstimate(
            flops=2 * micros * rows * D_VIS * WIDTH * units,
            bytes_accessed=units * D_VIS * WIDTH * 2,
            transcendentals=micros * rows * rows * HEADS,
        ),
        name=name,
    )(*args)


def swap(block, bit):
    size = lax.axis_size("dp")
    return lax.ppermute(block, "dp", [(j, j ^ bit) for j in range(size)])


def between(block, from_first):
    size = lax.axis_size("phase")
    pairs = [(j, j ^ 1) for j in range(size) if (j % 4 in (1, 2)) == from_first]
    return lax.ppermute(block, "phase", pairs)


def unit_out(block):
    return block.reshape(80, 2, WIDTH).transpose(1, 0, 2).reshape(160, WIDTH)


def units_qkv(block):
    return block.reshape(160, 3, WIDTH).transpose(1, 0, 2)


def staged_body(patches, window_ids, norm_gain, w_qkv, w_out, merge_gain):
    tie = lax.optimization_barrier
    place = lax.axis_index("phase") % 4
    me = lax.axis_index("dp").astype(jnp.int32).reshape(1)
    first = (place == 1) | (place == 2)

    def pick(array, one, two):
        return lax.dynamic_index_in_dim(array, jnp.where(first, one, two), 0, keepdims=False)

    chunk_a = jnp.concatenate([units_qkv(pick(w_qkv, 0, 2)), unit_out(pick(w_out, 0, 1))[None]])
    chunk_b = units_qkv(pick(w_qkv, 1, 3))
    chunk_c = jnp.stack([unit_out(w_out[2]), unit_out(w_out[3])])
    gains_1 = norm_gain[:2].reshape(2, 1, D_VIS)
    gains_2 = norm_gain[2:].reshape(2, 1, D_VIS)
    merge = merge_gain.reshape(1, D_VIS)

    ax, ay = swap(chunk_a, 2), swap(chunk_a, 4)
    other_ids = lax.ppermute(
        window_ids, "phase", [(j, j ^ 1) for j in range(lax.axis_size("phase"))]
    )
    other = between(patches, False)
    ax, ay, chunk_b = tie((ax, ay, chunk_b))
    ad = [swap(ax[:, :80], 4), swap(ay[:, 80:], 2)]
    bx, by = swap(chunk_b, 2), swap(chunk_b, 4)
    blocks_a = [chunk_a, ax, ay] + ad
    blocks_a += [swap(block, 1) for block in blocks_a]

    bx, by = tie((bx, by))
    bd = [swap(bx[:, :80], 4), swap(by[:, 80:], 2)]
    blocks_b = [chunk_b, bx, by] + bd
    blocks_b += [swap(block, 1) for block in blocks_b]

    bd[0], bd[1], chunk_c = tie((bd[0], bd[1], chunk_c))
    cx, cy = swap(chunk_c, 2), swap(chunk_c, 4)
    cx, cy = tie((cx, cy))
    cd = [swap(cx[:, :80], 4), swap(cy[:, 80:], 2)]
    blocks_c = [chunk_c, cx, cy] + cd
    blocks_c += [swap(block, 1) for block in blocks_c]

    acts = run_stage(
        "section_0", [("att", 0, 0), ("out", 3)],
        [(0, 0, False), (0, 1, False), (0, 2, False), (0, 3, True)],
        me, [(patches, 0), (other, 0)], None, [window_ids, other_ids], gains_1, merge, [blocks_a],
    )
    acts_far = between(acts, True)
    contexts = []
    for m, ids in enumerate((window_ids, other_ids)):
        context = run_stage(
            "attention_1", [("att", 1, 0)], [(0, 0, False), (0, 1, False), (0, 2, False)],
            me, [(acts, 128 * m)], None, [ids], gains_1, merge, [blocks_b],
        )
        contexts.append(between(context, True))
    steps = [("out", 0), ("att", 0, 1), ("out", 4), ("att", 1, 5), ("out", 8), ("norm",)]
    loads = [(0, 3, True), (0, 0, False), (0, 1, False), (0, 2, False), (2, 0, True),
             (1, 0, False), (1, 1, False), (1, 2, False), (2, 1, True)]
    results = []
    for m, ids in enumerate((other_ids, window_ids)):
        results.append(
            run_stage(
                "sections_2_3", steps, loads, me, [(acts_far, 128 * m)], contexts[m], [ids],
                gains_2, merge, [blocks_a, blocks_b, blocks_c],
            )
        )
    back = between(results[0], False)
    return jnp.where(first, back, results[1])


def plain_section(acts, marks, gain, weight_qkv, weight_out):
    rows = acts.shape[0]
    values_f = acts.astype(jnp.float32)
    normed = normed_rows(values_f, gain).astype(jnp.bfloat16)
    qkv = jnp.dot(normed, weight_qkv, preferred_element_type=jnp.float32).astype(jnp.bfloat16)
    query, keys, vals = (
        qkv[:, i * WIDTH : (i + 1) * WIDTH].reshape(rows, HEADS, HEAD_DIM) for i in range(3)
    )
    scores = jnp.einsum(
        "qhd,khd->hqk", query, keys, preferred_element_type=jnp.float32
    ) * HEAD_DIM ** (-0.5)
    same = marks[:, None] == marks[None, :]
    scores = jnp.where(same[None], scores, jnp.float32(NEG))
    probs = jax.nn.softmax(scores, axis=-1).astype(jnp.bfloat16)
    context = jnp.einsum("hqk,khd->qhd", probs, vals, preferred_element_type=jnp.float32)
    context = context.astype(jnp.bfloat16).reshape(rows, WIDTH)
    update = jnp.dot(context, weight_out, preferred_element_type=jnp.float32)
    return (values_f + update).astype(jnp.bfloat16)


def plain_body(patches, window_ids, norm_gain, w_qkv, w_out, merge_gain):
    acts = patches
    for k in range(w_qkv.shape[0]):
        local_qkv, local_out, acts = lax.optimization_barrier((w_qkv[k], w_out[k], acts))
        weight_qkv = lax.all_gather(local_qkv, "dp", axis=0, tiled=True)
        weight_out = lax.all_gather(local_out, "dp", axis=0, tiled=True)
        acts = plain_section(acts, window_ids[0], norm_gain[k], weight_qkv, weight_out)
    final = normed_rows(acts.astype(jnp.float32), merge_gain).astype(jnp.bfloat16)
    return final.reshape(-1, 4 * D_VIS)


def body(patches, window_ids, norm_gain, w_qkv, w_out, merge_gain):
    staged = lax.axis_size("dp") == 8 and lax.axis_size("phase") % 4 == 0
    run = staged_body if staged else plain_body
    return run(patches, window_ids, norm_gain, w_qkv, w_out, merge_gain)


def solution(mesh):
    in_specs = (
        P(("dp", "phase"), None),
        P(("dp", "phase"), None),
        P(),
        P(None, "dp", None),
        P(None, "dp", None),
        P(),
    )
    out_specs = P(("dp", "phase"), None)
    return jax.shard_map(body, mesh=mesh, in_specs=in_specs, out_specs=out_specs, check_vma=False)
```

```python
import functools

import jax
import jax.numpy as jnp
from jax import lax
from jax.experimental import pallas as pl
from jax.experimental.pallas import tpu as pltpu
from jax.sharding import PartitionSpec as P

D_VIS = 1280
HEADS = 8
HEAD_DIM = 80
WIDTH = HEADS * HEAD_DIM
SECTIONS = 4
LANES = 128
EPS = 1e-06
NEG = -1e30


def normed_rows(values, gain):
    scale = lax.rsqrt(jnp.mean(values * values, axis=-1, keepdims=True) + EPS)
    return values * scale * gain


def attend(qkv, row_ids):
    query, keys, vals = qkv
    rows = query.shape[0]
    across = jnp.broadcast_to(row_ids, (rows, rows))
    same = across == across.T
    lane = lax.broadcasted_iota(jnp.int32, (rows, LANES), 1)
    tiles = [None] * (WIDTH // LANES)
    for head in range(HEADS):
        first, last = head * HEAD_DIM, (head + 1) * HEAD_DIM
        low, high = first // LANES, -(-last // LANES)
        span = slice(low * LANES, high * LANES)
        inside = []
        for tile in range(low, high):
            place = lane + tile * LANES
            inside.append((place >= first) & (place < last))
        part = jnp.concatenate(
            [
                jnp.where(mask, query[:, (low + i) * LANES : (low + i + 1) * LANES], 0)
                for i, mask in enumerate(inside)
            ],
            axis=1,
        )
        scores = lax.dot_general(
            part, keys[:, span], (((1,), (1,)), ((), ())), preferred_element_type=jnp.float32
        )
        scores = jnp.where(same, scores * HEAD_DIM ** (-0.5), NEG)
        weights = jnp.exp(scores - jnp.max(scores, axis=-1, keepdims=True))
        probs = weights * (1.0 / jnp.sum(weights, axis=-1, keepdims=True))
        mixed = jnp.dot(
            probs.astype(jnp.bfloat16), vals[:, span], preferred_element_type=jnp.float32
        )
        for i, mask in enumerate(inside):
            kept = jnp.where(mask, mixed[:, i * LANES : (i + 1) * LANES], 0.0)
            tile = low + i
            tiles[tile] = kept if tiles[tile] is None else tiles[tile] + kept
    return jnp.concatenate(tiles, axis=1).astype(jnp.bfloat16)


def stage_kernel(steps, n_weights, micros, acts_parts, with_ctx, *refs):
    refs = list(refs)
    acts_refs = [refs.pop(0) for _ in acts_parts]
    ctx_ref = refs.pop(0) if with_ctx else None
    ids_refs = [refs.pop(0) for _ in range(micros)]
    gain_ref = refs.pop(0)
    merge_ref = refs.pop(0)
    held = [refs.pop(0) for _ in range(n_weights)]
    sheets, flow = refs.pop(), refs.pop()
    out_refs = refs

    rows = 128
    for m, (ref, row) in enumerate(zip(acts_refs, acts_parts)):
        flow[m * rows : (m + 1) * rows] = ref[row : row + rows].astype(jnp.float32)
    ctx = ctx_ref[...] if with_ctx else None
    for step in steps:
        if step[0] == "att":
            normed = normed_rows(flow[...], gain_ref[step[1]]).astype(jnp.bfloat16)
            qkv = [
                jnp.dot(
                    normed, held[step[2]][step[3] + i], preferred_element_type=jnp.float32
                ).astype(jnp.bfloat16)
                for i in range(3)
            ]
            parts = [
                attend([part[m * rows : (m + 1) * rows] for part in qkv], ids_refs[m][...])
                for m in range(micros)
            ]
            ctx = parts[0] if micros == 1 else jnp.concatenate(parts, axis=0)
        elif step[0] == "out":
            for half in range(2):
                at = slice(half * WIDTH, (half + 1) * WIDTH)
                moved = jnp.dot(
                    ctx, held[step[1]][step[2], half * WIDTH : (half + 1) * WIDTH],
                    preferred_element_type=jnp.float32,
                )
                flow[:, at] = (flow[:, at] + moved).astype(jnp.bfloat16).astype(jnp.float32)
        else:
            final = normed_rows(flow[...], merge_ref[...])
            for tile in range(D_VIS // LANES):
                sheets[tile] = final[:, tile * LANES : (tile + 1) * LANES]
            for i in range(4):
                for tile in range(D_VIS // LANES):
                    at = i * D_VIS + tile * LANES
                    out_refs[0][:, at : at + LANES] = sheets[
                        tile, pl.ds(i, rows // 4, stride=4), :
                    ].astype(jnp.bfloat16)
    if steps[-1][0] == "att":
        out_refs[-1][...] = ctx
    if steps[-1][0] != "norm" and len(steps) > 1:
        out_refs[0][...] = flow[...].astype(jnp.bfloat16)


def run_stage(name, steps, acts, ctx, ids, gains, merge, weights):
    micros = len(acts)
    rows = 128
    shapes = []
    if steps[-1][0] == "norm":
        shapes.append((rows // 4, 4 * D_VIS))
    elif len(steps) > 1:
        shapes.append((micros * rows, D_VIS))
    if steps[-1][0] == "att":
        shapes.append((micros * rows, WIDTH))
    kernel = functools.partial(
        stage_kernel, steps, len(weights), micros, [row for _, row in acts], ctx is not None
    )
    vmem = pl.BlockSpec(memory_space=pltpu.VMEM)
    args = [a for a, _ in acts] + ([ctx] if ctx is not None else []) + list(ids)
    args += [gains, merge] + list(weights)
    units = sum({"att": 3, "out": 1, "norm": 0}[step[0]] for step in steps)
    return pl.pallas_call(
        kernel,
        out_shape=[jax.ShapeDtypeStruct(shape, jnp.bfloat16) for shape in shapes],
        in_specs=[vmem] * len(args),
        out_specs=[vmem] * len(shapes),
        scratch_shapes=[
            pltpu.VMEM((micros * rows, D_VIS), jnp.float32),
            pltpu.VMEM((D_VIS // LANES, rows, LANES), jnp.float32),
        ],
        compiler_params=pltpu.CompilerParams(vmem_limit_bytes=8 * 1024 * 1024),
        cost_estimate=pl.CostEstimate(
            flops=2 * micros * rows * D_VIS * WIDTH * units,
            bytes_accessed=units * D_VIS * WIDTH * 2,
            transcendentals=micros * rows * rows * HEADS,
        ),
        name=name,
    )(*args)


def assemble_kernel(units, outs, pieces, *refs):
    whole = refs[-1]
    me = lax.axis_index("dp")
    for (first, distance, start, size), block in zip(pieces, refs[:-1]):
        owner = jnp.bitwise_xor(me, distance)
        for unit in range(units):
            if unit not in outs:
                where = pl.multiple_of(owner * 160 + start, 16)
                whole[unit, pl.ds(where, size)] = block[first + unit]
            else:
                for half in range(start // 80, (start + size) // 80):
                    where = pl.multiple_of(owner * 80 + half * WIDTH, 16)
                    at = half * 80 - start
                    whole[unit, pl.ds(where, 80)] = block[first + unit, at : at + 80]


def assemble(name, units, outs, pieces):
    vmem = pl.BlockSpec(memory_space=pltpu.VMEM)
    return pl.pallas_call(
        functools.partial(assemble_kernel, units, outs, [piece[1:] for piece in pieces]),
        out_shape=jax.ShapeDtypeStruct((units, D_VIS, WIDTH), jnp.bfloat16),
        in_specs=[vmem] * len(pieces),
        out_specs=vmem,
        compiler_params=pltpu.CompilerParams(vmem_limit_bytes=8 * 1024 * 1024),
        name=name,
    )(*[piece[0] for piece in pieces])


def first_stage():
    place = lax.axis_index("phase") % 4
    return (place == 1) | (place == 2)


def pack_kernel(qkv, out, chunk_a, chunk_b, chunk_c, chunks):
    first = first_stage()
    picks = [jnp.where(first, one, two) for one, two in ((0, 2), (0, 1), (1, 3))]
    for i in range(3):
        at = slice(i * WIDTH, (i + 1) * WIDTH)
        chunk_a[i] = qkv[picks[0], :, at]
        chunk_b[i] = qkv[picks[2], :, at]
    for half in range(2):
        at = slice(half * WIDTH, (half + 1) * WIDTH)
        to = slice(half * 80, (half + 1) * 80)
        chunk_a[3, to] = out[picks[1], :, at]
        chunk_c[0, to] = out[2, :, at]
        chunk_c[1, to] = out[3, :, at]
    chunks[0:4] = chunk_a[...]
    chunks[4:7] = chunk_b[...]
    chunks[7:9] = chunk_c[...]


def pack(w_qkv, w_out):
    vmem = pl.BlockSpec(memory_space=pltpu.VMEM)
    return pl.pallas_call(
        pack_kernel,
        out_shape=[jax.ShapeDtypeStruct((n, 160, WIDTH), jnp.bfloat16) for n in (4, 3, 2, 9)],
        in_specs=[vmem] * 2,
        out_specs=[vmem] * 4,
        compiler_params=pltpu.CompilerParams(vmem_limit_bytes=8 * 1024 * 1024),
        name="pack",
    )(w_qkv, w_out)


def swap(block, bit):
    size = lax.axis_size("dp")
    return lax.ppermute(block, "dp", [(j, j ^ bit) for j in range(size)])


def across(block):
    size = lax.axis_size("phase")
    return lax.ppermute(block, "phase", [(j, j ^ 1) for j in range(size)])


def staged_body(patches, window_ids, norm_gain, w_qkv, w_out, merge_gain):
    tie = lax.optimization_barrier
    gains_1 = norm_gain[:2].reshape(2, 1, D_VIS)
    gains_2 = norm_gain[2:].reshape(2, 1, D_VIS)
    merge = merge_gain.reshape(1, D_VIS)

    def arranged(name, outs, own, own_other, first, x, y, d):
        pieces = [(own, 0, 0, 0, 160), (own_other, first, 1, 0, 160)]
        for distance, block, start in ((2, x, 0), (4, y, 0), (6, d[0], 0), (6, d[1], 80)):
            size = block.shape[1]
            pieces.append((block, 0, distance, start, size))
            pieces.append((swap(block, 1), 0, distance + 1, start, size))
        return assemble(name, own.shape[0], outs, pieces)

    chunk_a, chunk_b, chunk_c, chunks = pack(w_qkv, w_out)
    ax, ay = swap(chunk_a, 2), swap(chunk_a, 4)
    bx, by = swap(chunk_b, 2), swap(chunk_b, 4)
    other, other_ids = across(patches), across(window_ids)
    own_other = swap(chunks, 1)
    ax, ay, other, other_ids = tie((ax, ay, other, other_ids))
    ad = swap(ax[:, :80], 4), swap(ay[:, 80:], 2)
    bx, by, own_other = tie((bx, by, own_other))
    bd = swap(bx[:, :80], 4), swap(by[:, 80:], 2)

    weights_a = arranged("weights_a", (3,), chunk_a, own_other, 0, ax, ay, ad)
    acts = run_stage(
        "section_0", [("att", 0, 0, 0), ("out", 0, 3)], [(patches, 0), (other, 0)], None,
        [window_ids, other_ids], gains_1, merge, [weights_a],
    )[0]
    *bd, acts, chunk_c = tie((*bd, acts, chunk_c))
    cx, cy = swap(chunk_c, 2), swap(chunk_c, 4)
    weights_b = arranged("weights_b", (), chunk_b, own_other, 4, bx, by, bd)
    acts_far = across(acts)
    contexts = [
        run_stage(
            "attention_1", [("att", 1, 0, 0)], [(acts, 128 * m)], None, [ids], gains_1, merge,
            [weights_b],
        )[0]
        for m, ids in enumerate((window_ids, other_ids))
    ]
    contexts_far = [across(context) for context in contexts]
    cx, cy, _ = tie((cx, cy, contexts[1]))
    cd = swap(cx[:, :80], 4), swap(cy[:, 80:], 2)
    halfway = [
        run_stage(
            "section_2", [("out", 0, 3), ("att", 0, 0, 0)], [(acts_far, 128 * m)],
            contexts_far[m], [ids], gains_2, merge, [weights_a],
        )
        for m, ids in enumerate((other_ids, window_ids))
    ]
    weights_c = arranged("weights_c", (0, 1), chunk_c, own_other, 7, cx, cy, cd)
    results = [
        run_stage(
            "section_3", [("out", 1, 0), ("att", 1, 0, 0), ("out", 1, 1), ("norm",)],
            [(halfway[m][0], 0)], halfway[m][1], [ids], gains_2, merge, [weights_b, weights_c],
        )[0]
        for m, ids in enumerate((other_ids, window_ids))
    ]
    back = across(results[0])
    return jnp.where(first_stage(), back, results[1])


def plain_section(acts, marks, gain, weight_qkv, weight_out):
    rows = acts.shape[0]
    values_f = acts.astype(jnp.float32)
    normed = normed_rows(values_f, gain).astype(jnp.bfloat16)
    qkv = jnp.dot(normed, weight_qkv, preferred_element_type=jnp.float32).astype(jnp.bfloat16)
    query, keys, vals = (
        qkv[:, i * WIDTH : (i + 1) * WIDTH].reshape(rows, HEADS, HEAD_DIM) for i in range(3)
    )
    scores = jnp.einsum(
        "qhd,khd->hqk", query, keys, preferred_element_type=jnp.float32
    ) * HEAD_DIM ** (-0.5)
    same = marks[:, None] == marks[None, :]
    scores = jnp.where(same[None], scores, jnp.float32(NEG))
    probs = jax.nn.softmax(scores, axis=-1).astype(jnp.bfloat16)
    context = jnp.einsum("hqk,khd->qhd", probs, vals, preferred_element_type=jnp.float32)
    context = context.astype(jnp.bfloat16).reshape(rows, WIDTH)
    update = jnp.dot(context, weight_out, preferred_element_type=jnp.float32)
    return (values_f + update).astype(jnp.bfloat16)


def plain_body(patches, window_ids, norm_gain, w_qkv, w_out, merge_gain):
    acts = patches
    for k in range(w_qkv.shape[0]):
        local_qkv, local_out, acts = lax.optimization_barrier((w_qkv[k], w_out[k], acts))
        weight_qkv = lax.all_gather(local_qkv, "dp", axis=0, tiled=True)
        weight_out = lax.all_gather(local_out, "dp", axis=0, tiled=True)
        acts = plain_section(acts, window_ids[0], norm_gain[k], weight_qkv, weight_out)
    final = normed_rows(acts.astype(jnp.float32), merge_gain).astype(jnp.bfloat16)
    return final.reshape(-1, 4 * D_VIS)


def body(patches, window_ids, norm_gain, w_qkv, w_out, merge_gain):
    staged = lax.axis_size("dp") == 8 and lax.axis_size("phase") % 4 == 0
    run = staged_body if staged else plain_body
    return run(patches, window_ids, norm_gain, w_qkv, w_out, merge_gain)


def solution(mesh):
    in_specs = (
        P(("dp", "phase"), None),
        P(("dp", "phase"), None),
        P(),
        P(None, "dp", None),
        P(None, "dp", None),
        P(),
    )
    out_specs = P(("dp", "phase"), None)
    return jax.shard_map(body, mesh=mesh, in_specs=in_specs, out_specs=out_specs, check_vma=False)
```

```python
import functools

import jax
import jax.numpy as jnp
from jax import lax
from jax.experimental import pallas as pl
from jax.experimental.pallas import tpu as pltpu
from jax.sharding import PartitionSpec as P

D_VIS = 1280
HEADS = 8
HEAD_DIM = 80
WIDTH = HEADS * HEAD_DIM
SECTIONS = 4
LANES = 128
EPS = 1e-06
NEG = -1e30
SMALL = pl.CostEstimate(flops=1, bytes_accessed=1, transcendentals=1)


def normed_rows(values, gain):
    scale = lax.rsqrt(jnp.mean(values * values, axis=-1, keepdims=True) + EPS)
    return values * scale * gain


def attend(qkv, row_ids):
    query, keys, vals = qkv
    rows = query.shape[0]
    across = jnp.broadcast_to(row_ids, (rows, rows))
    same = across == across.T
    lane = lax.broadcasted_iota(jnp.int32, (rows, LANES), 1)
    tiles = [None] * (WIDTH // LANES)
    for head in range(HEADS):
        first, last = head * HEAD_DIM, (head + 1) * HEAD_DIM
        low, high = first // LANES, -(-last // LANES)
        span = slice(low * LANES, high * LANES)
        inside = []
        for tile in range(low, high):
            place = lane + tile * LANES
            inside.append((place >= first) & (place < last))
        part = jnp.concatenate(
            [
                jnp.where(mask, query[:, (low + i) * LANES : (low + i + 1) * LANES], 0)
                for i, mask in enumerate(inside)
            ],
            axis=1,
        )
        scores = lax.dot_general(
            part, keys[:, span], (((1,), (1,)), ((), ())), preferred_element_type=jnp.float32
        )
        scores = jnp.where(same, scores * HEAD_DIM ** (-0.5), NEG)
        weights = jnp.exp(scores - jnp.max(scores, axis=-1, keepdims=True))
        probs = weights * (1.0 / jnp.sum(weights, axis=-1, keepdims=True))
        mixed = jnp.dot(
            probs.astype(jnp.bfloat16), vals[:, span], preferred_element_type=jnp.float32
        )
        for i, mask in enumerate(inside):
            kept = jnp.where(mask, mixed[:, i * LANES : (i + 1) * LANES], 0.0)
            tile = low + i
            tiles[tile] = kept if tiles[tile] is None else tiles[tile] + kept
    return jnp.concatenate(tiles, axis=1).astype(jnp.bfloat16)


def stage_kernel(stage, *refs):
    pl.when(first_stage() == (stage == 1))(functools.partial(two_sections, stage, *refs))


def two_sections(stage, acts_ref, ids_ref, gain_ref, merge_ref, one_ref, two_ref, out_ref, flow, sheets):
    rows = flow.shape[0]
    flow[...] = acts_ref[...].astype(jnp.float32)
    for i, held in enumerate((one_ref, two_ref)):
        normed = normed_rows(flow[...], gain_ref[2 * stage - 2 + i]).astype(jnp.bfloat16)
        qkv = [
            jnp.dot(normed, held[j], preferred_element_type=jnp.float32).astype(jnp.bfloat16)
            for j in range(3)
        ]
        context = attend(qkv, ids_ref[...])
        for half in range(2):
            at = slice(half * WIDTH, (half + 1) * WIDTH)
            moved = jnp.dot(context, held[3, at], preferred_element_type=jnp.float32)
            flow[:, at] = (flow[:, at] + moved).astype(jnp.bfloat16).astype(jnp.float32)
    if stage == 1:
        out_ref[...] = flow[...].astype(jnp.bfloat16)
    else:
        final = normed_rows(flow[...], merge_ref[...])
        for tile in range(D_VIS // LANES):
            sheets[tile] = final[:, tile * LANES : (tile + 1) * LANES]
        for i in range(4):
            for tile in range(D_VIS // LANES):
                at = i * D_VIS + tile * LANES
                out_ref[:, at : at + LANES] = sheets[
                    tile, pl.ds(i, rows // 4, stride=4), :
                ].astype(jnp.bfloat16)


def run_stage(stage, acts, ids, gains, merge, weights):
    rows = acts.shape[0]
    vmem = pl.BlockSpec(memory_space=pltpu.VMEM)
    args = [acts, ids, gains, merge] + list(weights)
    return pl.pallas_call(
        functools.partial(stage_kernel, stage),
        out_shape=jax.ShapeDtypeStruct(
            (rows, D_VIS) if stage == 1 else (rows // 4, 4 * D_VIS), jnp.bfloat16
        ),
        in_specs=[vmem] * len(args),
        out_specs=vmem,
        scratch_shapes=[
            pltpu.VMEM((rows, D_VIS), jnp.float32),
            pltpu.VMEM((D_VIS // LANES, rows, LANES), jnp.float32),
        ],
        compiler_params=pltpu.CompilerParams(vmem_limit_bytes=8 * 1024 * 1024),
        cost_estimate=SMALL,
        name=f"stage_{stage}",
    )(*args)


def assemble_kernel(first, *refs):
    *blocks, whole = refs
    me = lax.axis_index("dp")
    one = jnp.where(me % 2 == 0, 2, 4)
    distances = (0, 1, one, 6 - one, 6, 7 - one, 1 + one, 7)
    for i, (distance, block) in enumerate(zip(distances, blocks)):
        owner = jnp.bitwise_xor(me, distance)
        for unit in range(whole.shape[0]):
            at = unit + (first if i == 1 else 0)
            if unit < 3:
                whole[unit, pl.ds(pl.multiple_of(owner * 160, 16), 160)] = block[at]
            else:
                for half in range(2):
                    where = pl.multiple_of(owner * 80 + half * WIDTH, 16)
                    whole[unit, pl.ds(where, 80)] = block[at, half * 80 : half * 80 + 80]


def assemble(name, own, own_other, first, blocks, others):
    vmem = pl.BlockSpec(memory_space=pltpu.VMEM)
    return pl.pallas_call(
        functools.partial(assemble_kernel, first),
        out_shape=jax.ShapeDtypeStruct((own.shape[0], D_VIS, WIDTH), jnp.bfloat16),
        in_specs=[vmem] * 8,
        out_specs=vmem,
        compiler_params=pltpu.CompilerParams(vmem_limit_bytes=8 * 1024 * 1024),
        cost_estimate=SMALL,
        name=name,
    )(own, own_other, *blocks, *others)


def first_stage():
    place = lax.axis_index("phase") % 4
    return (place == 1) | (place == 2)


def pack_kernel(qkv, out, chunk_a, chunk_b, chunks):
    section = jnp.where(first_stage(), 0, 2)
    for which, chunk in enumerate((chunk_a, chunk_b)):
        for i in range(3):
            unit = qkv[section + which, :, i * WIDTH : (i + 1) * WIDTH]
            chunk[i] = unit
            chunks[4 * which + i] = unit
        for half in range(2):
            unit = out[section + which, :, half * WIDTH : (half + 1) * WIDTH]
            chunk[3, half * 80 : half * 80 + 80] = unit
            chunks[4 * which + 3, half * 80 : half * 80 + 80] = unit


def pack(w_qkv, w_out):
    vmem = pl.BlockSpec(memory_space=pltpu.VMEM)
    return pl.pallas_call(
        pack_kernel,
        out_shape=[jax.ShapeDtypeStruct((n, 160, WIDTH), jnp.bfloat16) for n in (4, 4, 8)],
        in_specs=[vmem] * 2,
        out_specs=[vmem] * 3,
        compiler_params=pltpu.CompilerParams(vmem_limit_bytes=8 * 1024 * 1024),
        cost_estimate=SMALL,
        name="pack",
    )(w_qkv, w_out)


def cores(block):
    return lax.ppermute(block, "dp", [(j, j ^ 1) for j in range(lax.axis_size("dp"))])


def plane(block, turn):
    pairs = [(j, j ^ (2 if j % 2 == turn else 4)) for j in range(lax.axis_size("dp"))]
    return lax.ppermute(block, "dp", pairs)


def across(block):
    size = lax.axis_size("phase")
    return lax.ppermute(block, "phase", [(j, j ^ 1) for j in range(size)])


def staged_body(patches, window_ids, norm_gain, w_qkv, w_out, merge_gain):
    tie = lax.optimization_barrier
    gains = norm_gain.reshape(SECTIONS, 1, D_VIS)
    merge = merge_gain.reshape(1, D_VIS)

    chunk_a, chunk_b, chunks = pack(w_qkv, w_out)
    a1, a2 = plane(chunk_a, 0), plane(chunk_a, 1)
    own_other = cores(chunks)
    own_other, b, theirs, their_ids = tie((own_other, chunk_b, patches, window_ids))
    b1, b2 = plane(b, 0), plane(b, 1)
    other, other_ids = across(theirs), across(their_ids)
    a1, a2, b1, b2, other, other_ids = tie((a1, a2, b1, b2, other, other_ids))
    a3, b3 = plane(a1, 1), plane(b2, 0)
    a1_other, a2_other, b1_other, b2_other = (cores(block) for block in (a1, a2, b1, b2))
    a3, b3, a1_other, a2_other, b1_other, b2_other = tie(
        (a3, b3, a1_other, a2_other, b1_other, b2_other)
    )
    weights = [
        assemble(
            "weights_a", chunk_a, own_other, 0, (a1, a2, a3), (a1_other, a2_other, cores(a3))
        ),
        assemble(
            "weights_b", chunk_b, own_other, 4, (b1, b2, b3), (b1_other, b2_other, cores(b3))
        ),
    ]

    half_own = run_stage(1, patches, window_ids, gains, merge, weights)
    half_own_far = across(half_own)
    half_own, other = tie((half_own, other))
    half_other = run_stage(1, other, other_ids, gains, merge, weights)
    half_other_far = across(half_other)
    result_other = run_stage(2, half_own_far, other_ids, gains, merge, weights)
    back = across(result_other)
    half_other_far, result_other = tie((half_other_far, result_other))
    result_own = run_stage(2, half_other_far, window_ids, gains, merge, weights)
    return jnp.where(first_stage(), back, result_own)


def plain_section(acts, marks, gain, weight_qkv, weight_out):
    rows = acts.shape[0]
    values_f = acts.astype(jnp.float32)
    normed = normed_rows(values_f, gain).astype(jnp.bfloat16)
    qkv = jnp.dot(normed, weight_qkv, preferred_element_type=jnp.float32).astype(jnp.bfloat16)
    query, keys, vals = (
        qkv[:, i * WIDTH : (i + 1) * WIDTH].reshape(rows, HEADS, HEAD_DIM) for i in range(3)
    )
    scores = jnp.einsum(
        "qhd,khd->hqk", query, keys, preferred_element_type=jnp.float32
    ) * HEAD_DIM ** (-0.5)
    same = marks[:, None] == marks[None, :]
    scores = jnp.where(same[None], scores, jnp.float32(NEG))
    probs = jax.nn.softmax(scores, axis=-1).astype(jnp.bfloat16)
    context = jnp.einsum("hqk,khd->qhd", probs, vals, preferred_element_type=jnp.float32)
    context = context.astype(jnp.bfloat16).reshape(rows, WIDTH)
    update = jnp.dot(context, weight_out, preferred_element_type=jnp.float32)
    return (values_f + update).astype(jnp.bfloat16)


def plain_body(patches, window_ids, norm_gain, w_qkv, w_out, merge_gain):
    acts = patches
    for k in range(w_qkv.shape[0]):
        local_qkv, local_out, acts = lax.optimization_barrier((w_qkv[k], w_out[k], acts))
        weight_qkv = lax.all_gather(local_qkv, "dp", axis=0, tiled=True)
        weight_out = lax.all_gather(local_out, "dp", axis=0, tiled=True)
        acts = plain_section(acts, window_ids[0], norm_gain[k], weight_qkv, weight_out)
    final = normed_rows(acts.astype(jnp.float32), merge_gain).astype(jnp.bfloat16)
    return final.reshape(-1, 4 * D_VIS)


def body(patches, window_ids, norm_gain, w_qkv, w_out, merge_gain):
    staged = lax.axis_size("dp") == 8 and lax.axis_size("phase") % 4 == 0
    run = staged_body if staged else plain_body
    return run(patches, window_ids, norm_gain, w_qkv, w_out, merge_gain)


def solution(mesh):
    in_specs = (
        P(("dp", "phase"), None),
        P(("dp", "phase"), None),
        P(),
        P(None, "dp", None),
        P(None, "dp", None),
        P(),
    )
    out_specs = P(("dp", "phase"), None)
    return jax.shard_map(body, mesh=mesh, in_specs=in_specs, out_specs=out_specs, check_vma=False)
```

```python
import functools

import jax
import jax.numpy as jnp
from jax import lax
from jax.experimental import pallas as pl
from jax.experimental.pallas import tpu as pltpu
from jax.sharding import PartitionSpec as P

D_VIS = 1280
HEADS = 8
HEAD_DIM = 80
WIDTH = HEADS * HEAD_DIM
SECTIONS = 4
LANES = 128
EPS = 1e-06
NEG = -1e30
SMALL = pl.CostEstimate(flops=1, bytes_accessed=1, transcendentals=1)


def normed_rows(values, gain):
    scale = lax.rsqrt(jnp.mean(values * values, axis=-1, keepdims=True) + EPS)
    return values * scale * gain


def attend(qkv, row_ids):
    query, keys, vals = qkv
    rows = query.shape[0]
    across = jnp.broadcast_to(row_ids, (rows, rows))
    same = across == across.T
    lane = lax.broadcasted_iota(jnp.int32, (rows, LANES), 1)
    tiles = [None] * (WIDTH // LANES)
    for head in range(HEADS):
        first, last = head * HEAD_DIM, (head + 1) * HEAD_DIM
        low, high = first // LANES, -(-last // LANES)
        span = slice(low * LANES, high * LANES)
        inside = []
        for tile in range(low, high):
            place = lane + tile * LANES
            inside.append((place >= first) & (place < last))
        part = jnp.concatenate(
            [
                jnp.where(mask, query[:, (low + i) * LANES : (low + i + 1) * LANES], 0)
                for i, mask in enumerate(inside)
            ],
            axis=1,
        )
        scores = lax.dot_general(
            part, keys[:, span], (((1,), (1,)), ((), ())), preferred_element_type=jnp.float32
        )
        scores = jnp.where(same, scores * HEAD_DIM ** (-0.5), NEG)
        weights = jnp.exp(scores - jnp.max(scores, axis=-1, keepdims=True))
        probs = weights * (1.0 / jnp.sum(weights, axis=-1, keepdims=True))
        mixed = jnp.dot(
            probs.astype(jnp.bfloat16), vals[:, span], preferred_element_type=jnp.float32
        )
        for i, mask in enumerate(inside):
            kept = jnp.where(mask, mixed[:, i * LANES : (i + 1) * LANES], 0.0)
            tile = low + i
            tiles[tile] = kept if tiles[tile] is None else tiles[tile] + kept
    return jnp.concatenate(tiles, axis=1).astype(jnp.bfloat16)


def stage_kernel(stage, *refs):
    pl.when(first_stage() == (stage == 1))(functools.partial(two_sections, stage, *refs))


def two_sections(stage, acts_ref, ids_ref, gain_ref, merge_ref, one_ref, two_ref, out_ref, flow, sheets):
    rows = flow.shape[0]
    flow[...] = acts_ref[...].astype(jnp.float32)
    for i, held in enumerate((one_ref, two_ref)):
        normed = normed_rows(flow[...], gain_ref[2 * stage - 2 + i]).astype(jnp.bfloat16)
        qkv = [
            jnp.dot(normed, held[j], preferred_element_type=jnp.float32).astype(jnp.bfloat16)
            for j in range(3)
        ]
        context = attend(qkv, ids_ref[...])
        for half in range(2):
            at = slice(half * WIDTH, (half + 1) * WIDTH)
            moved = jnp.dot(context, held[3, at], preferred_element_type=jnp.float32)
            flow[:, at] = (flow[:, at] + moved).astype(jnp.bfloat16).astype(jnp.float32)
    if stage == 1:
        out_ref[...] = flow[...].astype(jnp.bfloat16)
    else:
        final = normed_rows(flow[...], merge_ref[...])
        for tile in range(D_VIS // LANES):
            sheets[tile] = final[:, tile * LANES : (tile + 1) * LANES]
        for i in range(4):
            for tile in range(D_VIS // LANES):
                at = i * D_VIS + tile * LANES
                out_ref[:, at : at + LANES] = sheets[
                    tile, pl.ds(i, rows // 4, stride=4), :
                ].astype(jnp.bfloat16)


def run_stage(stage, acts, ids, gains, merge, weights):
    rows = acts.shape[0]
    vmem = pl.BlockSpec(memory_space=pltpu.VMEM)
    args = [acts, ids, gains, merge] + list(weights)
    return pl.pallas_call(
        functools.partial(stage_kernel, stage),
        out_shape=jax.ShapeDtypeStruct(
            (rows, D_VIS) if stage == 1 else (rows // 4, 4 * D_VIS), jnp.bfloat16
        ),
        in_specs=[vmem] * len(args),
        out_specs=vmem,
        scratch_shapes=[
            pltpu.VMEM((rows, D_VIS), jnp.float32),
            pltpu.VMEM((D_VIS // LANES, rows, LANES), jnp.float32),
        ],
        compiler_params=pltpu.CompilerParams(vmem_limit_bytes=8 * 1024 * 1024),
        cost_estimate=SMALL,
        name=f"stage_{stage}",
    )(*args)


def assemble_kernel(first, *refs):
    *blocks, whole = refs
    me = lax.axis_index("dp")
    one = jnp.where(me % 2 == 0, 2, 4)
    distances = (0, 1, one, 6 - one, 6, 7 - one, 1 + one, 7)
    for i, (distance, block) in enumerate(zip(distances, blocks)):
        owner = jnp.bitwise_xor(me, distance)
        for unit in range(whole.shape[0]):
            at = unit + (first if i == 1 else 0)
            if unit < 3:
                whole[unit, pl.ds(pl.multiple_of(owner * 160, 16), 160)] = block[at]
            else:
                for half in range(2):
                    where = pl.multiple_of(owner * 80 + half * WIDTH, 16)
                    whole[unit, pl.ds(where, 80)] = block[at, half * 80 : half * 80 + 80]


def assemble(name, own, own_other, first, blocks, others):
    vmem = pl.BlockSpec(memory_space=pltpu.VMEM)
    return pl.pallas_call(
        functools.partial(assemble_kernel, first),
        out_shape=jax.ShapeDtypeStruct((own.shape[0], D_VIS, WIDTH), jnp.bfloat16),
        in_specs=[vmem] * 8,
        out_specs=vmem,
        compiler_params=pltpu.CompilerParams(vmem_limit_bytes=8 * 1024 * 1024),
        cost_estimate=SMALL,
        name=name,
    )(own, own_other, *blocks, *others)


def first_stage():
    place = lax.axis_index("phase") % 4
    return (place == 1) | (place == 2)


def pack_kernel(qkv, out, chunk_a, chunk_b, chunks):
    section = jnp.where(first_stage(), 0, 2)
    for which, chunk in enumerate((chunk_a, chunk_b)):
        for i in range(3):
            unit = qkv[section + which, :, i * WIDTH : (i + 1) * WIDTH]
            chunk[i] = unit
            chunks[4 * which + i] = unit
        for half in range(2):
            unit = out[section + which, :, half * WIDTH : (half + 1) * WIDTH]
            chunk[3, half * 80 : half * 80 + 80] = unit
            chunks[4 * which + 3, half * 80 : half * 80 + 80] = unit


def pack(w_qkv, w_out):
    vmem = pl.BlockSpec(memory_space=pltpu.VMEM)
    return pl.pallas_call(
        pack_kernel,
        out_shape=[jax.ShapeDtypeStruct((n, 160, WIDTH), jnp.bfloat16) for n in (4, 4, 8)],
        in_specs=[vmem] * 2,
        out_specs=[vmem] * 3,
        compiler_params=pltpu.CompilerParams(vmem_limit_bytes=8 * 1024 * 1024),
        cost_estimate=SMALL,
        name="pack",
    )(w_qkv, w_out)


def choose_kernel(one_ref, two_ref, out_ref):
    first = first_stage()

    @pl.when(first)
    def _():
        out_ref[...] = one_ref[...]

    @pl.when(jnp.logical_not(first))
    def _():
        out_ref[...] = two_ref[...]


def choose(one, two):
    vmem = pl.BlockSpec(memory_space=pltpu.VMEM)
    return pl.pallas_call(
        choose_kernel,
        out_shape=jax.ShapeDtypeStruct(one.shape, one.dtype),
        in_specs=[vmem] * 2,
        out_specs=vmem,
        compiler_params=pltpu.CompilerParams(vmem_limit_bytes=8 * 1024 * 1024),
        cost_estimate=SMALL,
        name="choose",
    )(one, two)


def cores(block):
    return lax.ppermute(block, "dp", [(j, j ^ 1) for j in range(lax.axis_size("dp"))])


def plane(block, turn):
    pairs = [(j, j ^ (2 if j % 2 == turn else 4)) for j in range(lax.axis_size("dp"))]
    return lax.ppermute(block, "dp", pairs)


def across(block):
    size = lax.axis_size("phase")
    return lax.ppermute(block, "phase", [(j, j ^ 1) for j in range(size)])


def staged_body(patches, window_ids, norm_gain, w_qkv, w_out, merge_gain):
    tie = lax.optimization_barrier
    gains = norm_gain.reshape(SECTIONS, 1, D_VIS)
    merge = merge_gain.reshape(1, D_VIS)

    chunk_a, chunk_b, chunks = pack(w_qkv, w_out)
    a1, a2 = plane(chunk_a, 0), plane(chunk_a, 1)
    own_other = cores(chunks)
    own_other, b, theirs, their_ids = tie((own_other, chunk_b, patches, window_ids))
    b1, b2 = plane(b, 0), plane(b, 1)
    other, other_ids = across(theirs), across(their_ids)
    a1, a2, b1, b2, other, other_ids = tie((a1, a2, b1, b2, other, other_ids))
    a3, b3 = plane(a1, 1), plane(b2, 0)
    a1_other, a2_other, b1_other, b2_other = (cores(block) for block in (a1, a2, b1, b2))
    a3, b3, a1_other, a2_other, b1_other, b2_other = tie(
        (a3, b3, a1_other, a2_other, b1_other, b2_other)
    )
    weights = [
        assemble(
            "weights_a", chunk_a, own_other, 0, (a1, a2, a3), (a1_other, a2_other, cores(a3))
        ),
        assemble(
            "weights_b", chunk_b, own_other, 4, (b1, b2, b3), (b1_other, b2_other, cores(b3))
        ),
    ]

    half_own = run_stage(1, patches, window_ids, gains, merge, weights)
    half_own_far = across(half_own)
    half_own, other = tie((half_own, other))
    half_other = run_stage(1, other, other_ids, gains, merge, weights)
    half_other_far = across(half_other)
    result_other = run_stage(2, half_own_far, other_ids, gains, merge, weights)
    back = across(result_other)
    half_other_far, result_other = tie((half_other_far, result_other))
    result_own = run_stage(2, half_other_far, window_ids, gains, merge, weights)
    return choose(back, result_own)


def plain_section(acts, marks, gain, weight_qkv, weight_out):
    rows = acts.shape[0]
    values_f = acts.astype(jnp.float32)
    normed = normed_rows(values_f, gain).astype(jnp.bfloat16)
    qkv = jnp.dot(normed, weight_qkv, preferred_element_type=jnp.float32).astype(jnp.bfloat16)
    query, keys, vals = (
        qkv[:, i * WIDTH : (i + 1) * WIDTH].reshape(rows, HEADS, HEAD_DIM) for i in range(3)
    )
    scores = jnp.einsum(
        "qhd,khd->hqk", query, keys, preferred_element_type=jnp.float32
    ) * HEAD_DIM ** (-0.5)
    same = marks[:, None] == marks[None, :]
    scores = jnp.where(same[None], scores, jnp.float32(NEG))
    probs = jax.nn.softmax(scores, axis=-1).astype(jnp.bfloat16)
    context = jnp.einsum("hqk,khd->qhd", probs, vals, preferred_element_type=jnp.float32)
    context = context.astype(jnp.bfloat16).reshape(rows, WIDTH)
    update = jnp.dot(context, weight_out, preferred_element_type=jnp.float32)
    return (values_f + update).astype(jnp.bfloat16)


def plain_body(patches, window_ids, norm_gain, w_qkv, w_out, merge_gain):
    acts = patches
    for k in range(w_qkv.shape[0]):
        local_qkv, local_out, acts = lax.optimization_barrier((w_qkv[k], w_out[k], acts))
        weight_qkv = lax.all_gather(local_qkv, "dp", axis=0, tiled=True)
        weight_out = lax.all_gather(local_out, "dp", axis=0, tiled=True)
        acts = plain_section(acts, window_ids[0], norm_gain[k], weight_qkv, weight_out)
    final = normed_rows(acts.astype(jnp.float32), merge_gain).astype(jnp.bfloat16)
    return final.reshape(-1, 4 * D_VIS)


def body(patches, window_ids, norm_gain, w_qkv, w_out, merge_gain):
    staged = lax.axis_size("dp") == 8 and lax.axis_size("phase") % 4 == 0
    run = staged_body if staged else plain_body
    return run(patches, window_ids, norm_gain, w_qkv, w_out, merge_gain)


def solution(mesh):
    in_specs = (
        P(("dp", "phase"), None),
        P(("dp", "phase"), None),
        P(),
        P(None, "dp", None),
        P(None, "dp", None),
        P(),
    )
    out_specs = P(("dp", "phase"), None)
    return jax.shard_map(body, mesh=mesh, in_specs=in_specs, out_specs=out_specs, check_vma=False)
```

```python
import functools

import jax
import jax.numpy as jnp
from jax import lax
from jax.experimental import pallas as pl
from jax.experimental.pallas import tpu as pltpu
from jax.sharding import PartitionSpec as P

D_VIS = 1280
HEADS = 8
HEAD_DIM = 80
WIDTH = HEADS * HEAD_DIM
SECTIONS = 4
LANES = 128
EPS = 1e-06
NEG = -1e30
SMALL = pl.CostEstimate(flops=1, bytes_accessed=1, transcendentals=1)


def normed_rows(values, gain):
    scale = lax.rsqrt(jnp.mean(values * values, axis=-1, keepdims=True) + EPS)
    return values * scale * gain


def attend(qkv, row_ids):
    query, keys, vals = qkv
    rows = query.shape[0]
    across = jnp.broadcast_to(row_ids, (rows, rows))
    same = across == across.T
    lane = lax.broadcasted_iota(jnp.int32, (rows, LANES), 1)
    tiles = [None] * (WIDTH // LANES)
    for head in range(HEADS):
        first, last = head * HEAD_DIM, (head + 1) * HEAD_DIM
        low, high = first // LANES, -(-last // LANES)
        span = slice(low * LANES, high * LANES)
        inside = []
        for tile in range(low, high):
            place = lane + tile * LANES
            inside.append((place >= first) & (place < last))
        part = jnp.concatenate(
            [
                jnp.where(mask, query[:, (low + i) * LANES : (low + i + 1) * LANES], 0)
                for i, mask in enumerate(inside)
            ],
            axis=1,
        )
        scores = lax.dot_general(
            part, keys[:, span], (((1,), (1,)), ((), ())), preferred_element_type=jnp.float32
        )
        scores = jnp.where(same, scores * HEAD_DIM ** (-0.5), NEG)
        weights = jnp.exp(scores - jnp.max(scores, axis=-1, keepdims=True))
        probs = weights * (1.0 / jnp.sum(weights, axis=-1, keepdims=True))
        mixed = jnp.dot(
            probs.astype(jnp.bfloat16), vals[:, span], preferred_element_type=jnp.float32
        )
        for i, mask in enumerate(inside):
            kept = jnp.where(mask, mixed[:, i * LANES : (i + 1) * LANES], 0.0)
            tile = low + i
            tiles[tile] = kept if tiles[tile] is None else tiles[tile] + kept
    return jnp.concatenate(tiles, axis=1).astype(jnp.bfloat16)


def stage_kernel(stage, *refs):
    pl.when(first_stage() == (stage == 1))(functools.partial(two_sections, stage, *refs))


def two_sections(stage, acts_ref, ids_ref, gain_ref, merge_ref, one_ref, two_ref, out_ref, flow, sheets):
    rows = flow.shape[0]
    flow[...] = acts_ref[...].astype(jnp.float32)
    for i, held in enumerate((one_ref, two_ref)):
        normed = normed_rows(flow[...], gain_ref[2 * stage - 2 + i]).astype(jnp.bfloat16)
        qkv = [
            jnp.dot(normed, held[j], preferred_element_type=jnp.float32).astype(jnp.bfloat16)
            for j in range(3)
        ]
        context = attend(qkv, ids_ref[...])
        for half in range(2):
            at = slice(half * WIDTH, (half + 1) * WIDTH)
            moved = jnp.dot(context, held[3, at], preferred_element_type=jnp.float32)
            flow[:, at] = (flow[:, at] + moved).astype(jnp.bfloat16).astype(jnp.float32)
    if stage == 1:
        out_ref[...] = flow[...].astype(jnp.bfloat16)
    else:
        final = normed_rows(flow[...], merge_ref[...])
        for tile in range(D_VIS // LANES):
            sheets[tile] = final[:, tile * LANES : (tile + 1) * LANES]
        for i in range(4):
            for tile in range(D_VIS // LANES):
                at = i * D_VIS + tile * LANES
                out_ref[:, at : at + LANES] = sheets[
                    tile, pl.ds(i, rows // 4, stride=4), :
                ].astype(jnp.bfloat16)


def run_stage(stage, acts, ids, gains, merge, weights):
    rows = acts.shape[0]
    vmem = pl.BlockSpec(memory_space=pltpu.VMEM)
    args = [acts, ids, gains, merge] + list(weights)
    return pl.pallas_call(
        functools.partial(stage_kernel, stage),
        out_shape=jax.ShapeDtypeStruct(
            (rows, D_VIS) if stage == 1 else (rows // 4, 4 * D_VIS), jnp.bfloat16
        ),
        in_specs=[vmem] * len(args),
        out_specs=vmem,
        scratch_shapes=[
            pltpu.VMEM((rows, D_VIS), jnp.float32),
            pltpu.VMEM((D_VIS // LANES, rows, LANES), jnp.float32),
        ],
        compiler_params=pltpu.CompilerParams(vmem_limit_bytes=8 * 1024 * 1024),
        cost_estimate=SMALL,
        name=f"stage_{stage}",
    )(*args)


def assemble_kernel(*refs):
    blocks, whole = refs[:-2], refs[-2:]
    turned = flipped()
    for swapped in (False, True):
        pl.when(turned == swapped)(
            functools.partial(put_in_order, blocks, whole[::-1] if swapped else whole)
        )


def put_in_order(blocks, whole):
    me = lax.axis_index("dp")
    one = jnp.where(me % 2 == 0, 2, 4)
    for which in range(2):
        for i, distance in enumerate((0, one, 6 - one, 6, 1, 7 - one, 1 + one, 7)):
            block = blocks[8 * which + i]
            first = 4 * which if block.shape[0] == 8 else 0
            owner = jnp.bitwise_xor(me, distance)
            for unit in range(3):
                where = pl.ds(pl.multiple_of(owner * 160, 16), 160)
                whole[which][unit, where] = block[first + unit]
            for half in range(2):
                where = pl.ds(pl.multiple_of(owner * 80 + half * WIDTH, 16), 80)
                whole[which][3, where] = block[first + 3, half * 80 : half * 80 + 80]


def assemble(p, q):
    vmem = pl.BlockSpec(memory_space=pltpu.VMEM)
    return pl.pallas_call(
        assemble_kernel,
        out_shape=[jax.ShapeDtypeStruct((4, D_VIS, WIDTH), jnp.bfloat16)] * 2,
        in_specs=[vmem] * 16,
        out_specs=[vmem] * 2,
        compiler_params=pltpu.CompilerParams(vmem_limit_bytes=8 * 1024 * 1024),
        cost_estimate=SMALL,
        name="assemble",
    )(*p, *q)


def choose_kernel(one_ref, two_ref, out_ref):
    first = first_stage()

    @pl.when(first)
    def _():
        out_ref[...] = one_ref[...]

    @pl.when(jnp.logical_not(first))
    def _():
        out_ref[...] = two_ref[...]


def first_stage():
    place = lax.axis_index("phase") % 4
    return (place == 1) | (place == 2)


def flipped():
    return lax.axis_index("phase") % 4 == 2


def pack_kernel(qkv, out, chunk_p, chunk_q, chunks):
    first = jnp.where(first_stage(), 0, 2)
    turned = jnp.where(flipped(), 1, 0)
    for which, chunk in enumerate((chunk_p, chunk_q)):
        section = first + jnp.bitwise_xor(turned, which)
        for i in range(3):
            unit = qkv[section, :, i * WIDTH : (i + 1) * WIDTH]
            chunk[i] = unit
            chunks[4 * which + i] = unit
        for half in range(2):
            unit = out[section, :, half * WIDTH : (half + 1) * WIDTH]
            chunk[3, half * 80 : half * 80 + 80] = unit
            chunks[4 * which + 3, half * 80 : half * 80 + 80] = unit


def pack(w_qkv, w_out):
    vmem = pl.BlockSpec(memory_space=pltpu.VMEM)
    return pl.pallas_call(
        pack_kernel,
        out_shape=[jax.ShapeDtypeStruct((n, 160, WIDTH), jnp.bfloat16) for n in (4, 4, 8)],
        in_specs=[vmem] * 2,
        out_specs=[vmem] * 3,
        compiler_params=pltpu.CompilerParams(vmem_limit_bytes=8 * 1024 * 1024),
        cost_estimate=SMALL,
        name="pack",
    )(w_qkv, w_out)


def choose(name, one, two):
    vmem = pl.BlockSpec(memory_space=pltpu.VMEM)
    return pl.pallas_call(
        choose_kernel,
        out_shape=jax.ShapeDtypeStruct(one.shape, one.dtype),
        in_specs=[vmem] * 2,
        out_specs=vmem,
        compiler_params=pltpu.CompilerParams(vmem_limit_bytes=8 * 1024 * 1024),
        cost_estimate=SMALL,
        name=name,
    )(one, two)


def cores(block):
    return lax.ppermute(block, "dp", [(j, j ^ 1) for j in range(lax.axis_size("dp"))])


def plane(block, turn):
    pairs = [(j, j ^ (2 if j % 2 == turn else 4)) for j in range(lax.axis_size("dp"))]
    return lax.ppermute(block, "dp", pairs)


def planes_or_plane(block):
    cores_, planes = lax.axis_size("dp"), lax.axis_size("phase")
    pairs = []
    for j in range(cores_):
        for z in range(planes):
            to = (j, z ^ 3) if z % 4 in (1, 2) else (j ^ (2 if j % 2 == 0 else 4), z)
            pairs.append((j * planes + z, to[0] * planes + to[1]))
    return lax.ppermute(block, ("dp", "phase"), pairs)


def across(block):
    size = lax.axis_size("phase")
    return lax.ppermute(block, "phase", [(j, j ^ 1) for j in range(size)])


def staged_body(patches, window_ids, norm_gain, w_qkv, w_out, merge_gain):
    tie = lax.optimization_barrier
    gains = norm_gain.reshape(SECTIONS, 1, D_VIS)
    merge = merge_gain.reshape(1, D_VIS)

    chunk_p, chunk_q, chunks = pack(w_qkv, w_out)
    p1, p2 = plane(chunk_p, 0), plane(chunk_p, 1)
    own_other = cores(chunks)
    own_other, late_q, theirs, their_ids = tie((own_other, chunk_q, patches, window_ids))
    q2 = plane(late_q, 1)
    other, other_ids = across(theirs), across(their_ids)
    p1, p2, q2, other, other_ids = tie((p1, p2, q2, other, other_ids))
    q1 = planes_or_plane(choose("relay", p1, chunk_q))
    p3, q3 = plane(p1, 1), plane(q2, 0)
    p1_other, p2_other, q2_other = cores(p1), cores(p2), cores(q2)
    q1, p3, q3, p1_other, p2_other, q2_other = tie((q1, p3, q3, p1_other, p2_other, q2_other))
    weights = assemble(
        (chunk_p, p1, p2, p3, own_other, p1_other, p2_other, cores(p3)),
        (chunk_q, q1, q2, q3, own_other, cores(q1), q2_other, cores(q3)),
    )

    half_own = run_stage(1, patches, window_ids, gains, merge, weights)
    half_own_far = across(half_own)
    half_own, other = tie((half_own, other))
    half_other = run_stage(1, other, other_ids, gains, merge, weights)
    half_other_far = across(half_other)
    result_other = run_stage(2, half_own_far, other_ids, gains, merge, weights)
    back = across(result_other)
    half_other_far, result_other = tie((half_other_far, result_other))
    result_own = run_stage(2, half_other_far, window_ids, gains, merge, weights)
    return choose("result", back, result_own)


def plain_section(acts, marks, gain, weight_qkv, weight_out):
    rows = acts.shape[0]
    values_f = acts.astype(jnp.float32)
    normed = normed_rows(values_f, gain).astype(jnp.bfloat16)
    qkv = jnp.dot(normed, weight_qkv, preferred_element_type=jnp.float32).astype(jnp.bfloat16)
    query, keys, vals = (
        qkv[:, i * WIDTH : (i + 1) * WIDTH].reshape(rows, HEADS, HEAD_DIM) for i in range(3)
    )
    scores = jnp.einsum(
        "qhd,khd->hqk", query, keys, preferred_element_type=jnp.float32
    ) * HEAD_DIM ** (-0.5)
    same = marks[:, None] == marks[None, :]
    scores = jnp.where(same[None], scores, jnp.float32(NEG))
    probs = jax.nn.softmax(scores, axis=-1).astype(jnp.bfloat16)
    context = jnp.einsum("hqk,khd->qhd", probs, vals, preferred_element_type=jnp.float32)
    context = context.astype(jnp.bfloat16).reshape(rows, WIDTH)
    update = jnp.dot(context, weight_out, preferred_element_type=jnp.float32)
    return (values_f + update).astype(jnp.bfloat16)


def plain_body(patches, window_ids, norm_gain, w_qkv, w_out, merge_gain):
    acts = patches
    for k in range(w_qkv.shape[0]):
        local_qkv, local_out, acts = lax.optimization_barrier((w_qkv[k], w_out[k], acts))
        weight_qkv = lax.all_gather(local_qkv, "dp", axis=0, tiled=True)
        weight_out = lax.all_gather(local_out, "dp", axis=0, tiled=True)
        acts = plain_section(acts, window_ids[0], norm_gain[k], weight_qkv, weight_out)
    final = normed_rows(acts.astype(jnp.float32), merge_gain).astype(jnp.bfloat16)
    return final.reshape(-1, 4 * D_VIS)


def body(patches, window_ids, norm_gain, w_qkv, w_out, merge_gain):
    staged = lax.axis_size("dp") == 8 and lax.axis_size("phase") % 4 == 0
    run = staged_body if staged else plain_body
    return run(patches, window_ids, norm_gain, w_qkv, w_out, merge_gain)


def solution(mesh):
    in_specs = (
        P(("dp", "phase"), None),
        P(("dp", "phase"), None),
        P(),
        P(None, "dp", None),
        P(None, "dp", None),
        P(),
    )
    out_specs = P(("dp", "phase"), None)
    return jax.shard_map(body, mesh=mesh, in_specs=in_specs, out_specs=out_specs, check_vma=False)
```

```python
import functools

import jax
import jax.numpy as jnp
from jax import lax
from jax.experimental import pallas as pl
from jax.experimental.pallas import tpu as pltpu
from jax.sharding import PartitionSpec as P

D_VIS = 1280
HEADS = 8
HEAD_DIM = 80
WIDTH = HEADS * HEAD_DIM
SECTIONS = 4
LANES = 128
EPS = 1e-06
NEG = -1e30
SMALL = pl.CostEstimate(flops=1, bytes_accessed=1, transcendentals=1)


def normed_rows(values, gain):
    scale = lax.rsqrt(jnp.mean(values * values, axis=-1, keepdims=True) + EPS)
    return values * scale * gain


def attend(qkv, row_ids):
    query, keys, vals = qkv
    rows = query.shape[0]
    across = jnp.broadcast_to(row_ids, (rows, rows))
    same = across == across.T
    lane = lax.broadcasted_iota(jnp.int32, (rows, LANES), 1)
    tiles = [None] * (WIDTH // LANES)
    for head in range(HEADS):
        first, last = head * HEAD_DIM, (head + 1) * HEAD_DIM
        low, high = first // LANES, -(-last // LANES)
        span = slice(low * LANES, high * LANES)
        inside = []
        for tile in range(low, high):
            place = lane + tile * LANES
            inside.append((place >= first) & (place < last))
        part = jnp.concatenate(
            [
                jnp.where(mask, query[:, (low + i) * LANES : (low + i + 1) * LANES], 0)
                for i, mask in enumerate(inside)
            ],
            axis=1,
        )
        scores = lax.dot_general(
            part, keys[:, span], (((1,), (1,)), ((), ())), preferred_element_type=jnp.float32
        )
        scores = jnp.where(same, scores * HEAD_DIM ** (-0.5), NEG)
        weights = jnp.exp(scores - jnp.max(scores, axis=-1, keepdims=True))
        probs = weights * (1.0 / jnp.sum(weights, axis=-1, keepdims=True))
        mixed = jnp.dot(
            probs.astype(jnp.bfloat16), vals[:, span], preferred_element_type=jnp.float32
        )
        for i, mask in enumerate(inside):
            kept = jnp.where(mask, mixed[:, i * LANES : (i + 1) * LANES], 0.0)
            tile = low + i
            tiles[tile] = kept if tiles[tile] is None else tiles[tile] + kept
    return jnp.concatenate(tiles, axis=1).astype(jnp.bfloat16)


def stage_kernel(stage, *refs):
    pl.when(first_stage() == (stage == 1))(functools.partial(two_sections, stage, *refs))


def two_sections(stage, acts_ref, ids_ref, gain_ref, merge_ref, one_ref, two_ref, out_ref, flow, sheets):
    rows = flow.shape[0]
    flow[...] = acts_ref[...].astype(jnp.float32)
    for i, held in enumerate((one_ref, two_ref)):
        normed = normed_rows(flow[...], gain_ref[2 * stage - 2 + i]).astype(jnp.bfloat16)
        qkv = [
            jnp.dot(normed, held[j], preferred_element_type=jnp.float32).astype(jnp.bfloat16)
            for j in range(3)
        ]
        context = attend(qkv, ids_ref[...])
        for half in range(2):
            at = slice(half * WIDTH, (half + 1) * WIDTH)
            moved = jnp.dot(context, held[3, at], preferred_element_type=jnp.float32)
            flow[:, at] = (flow[:, at] + moved).astype(jnp.bfloat16).astype(jnp.float32)
    if stage == 1:
        out_ref[...] = flow[...].astype(jnp.bfloat16)
    else:
        final = normed_rows(flow[...], merge_ref[...])
        for tile in range(D_VIS // LANES):
            sheets[tile] = final[:, tile * LANES : (tile + 1) * LANES]
        for i in range(4):
            for tile in range(D_VIS // LANES):
                at = i * D_VIS + tile * LANES
                out_ref[:, at : at + LANES] = sheets[
                    tile, pl.ds(i, rows // 4, stride=4), :
                ].astype(jnp.bfloat16)


def run_stage(stage, acts, ids, gains, merge, weights):
    rows = acts.shape[0]
    vmem = pl.BlockSpec(memory_space=pltpu.VMEM)
    args = [acts, ids, gains, merge] + list(weights)
    return pl.pallas_call(
        functools.partial(stage_kernel, stage),
        out_shape=jax.ShapeDtypeStruct(
            (rows, D_VIS) if stage == 1 else (rows // 4, 4 * D_VIS), jnp.bfloat16
        ),
        in_specs=[vmem] * len(args),
        out_specs=vmem,
        scratch_shapes=[
            pltpu.VMEM((rows, D_VIS), jnp.float32),
            pltpu.VMEM((D_VIS // LANES, rows, LANES), jnp.float32),
        ],
        compiler_params=pltpu.CompilerParams(vmem_limit_bytes=8 * 1024 * 1024),
        cost_estimate=SMALL,
        name=f"stage_{stage}",
    )(*args)


def assemble_kernel(stage, n_given, *refs):
    blocks, whole = refs[n_given : n_given + 16], refs[n_given + 16 :]
    turned, early = flipped(), first_stage()
    if stage == 2:
        pl.when(jnp.logical_not(early))(functools.partial(put_in_order, blocks, whole))
    else:
        for swapped in (False, True):
            pl.when(early & (turned == swapped))(
                functools.partial(put_in_order, blocks, whole[::-1] if swapped else whole)
            )


def put_in_order(blocks, whole):
    me = lax.axis_index("dp")
    one = jnp.where(me % 2 == 0, 2, 4)
    for which in range(2):
        for i, distance in enumerate((0, one, 6 - one, 6, 1, 7 - one, 1 + one, 7)):
            block = blocks[8 * which + i]
            first = 4 * which if block.shape[0] == 8 else 0
            owner = jnp.bitwise_xor(me, distance)
            for unit in range(3):
                where = pl.ds(pl.multiple_of(owner * 160, 16), 160)
                whole[which][unit, where] = block[first + unit]
            for half in range(2):
                where = pl.ds(pl.multiple_of(owner * 80 + half * WIDTH, 16), 80)
                whole[which][3, where] = block[first + 3, half * 80 : half * 80 + 80]


def assemble(stage, p, q, given=()):
    vmem = pl.BlockSpec(memory_space=pltpu.VMEM)
    return pl.pallas_call(
        functools.partial(assemble_kernel, stage, len(given)),
        out_shape=[jax.ShapeDtypeStruct((4, D_VIS, WIDTH), jnp.bfloat16)] * 2,
        in_specs=[vmem] * (len(given) + 16),
        out_specs=[vmem] * 2,
        input_output_aliases={i: i for i in range(len(given))},
        compiler_params=pltpu.CompilerParams(vmem_limit_bytes=8 * 1024 * 1024),
        cost_estimate=SMALL,
        name="assemble",
    )(*given, *p, *q)


def choose_kernel(one_ref, two_ref, out_ref):
    first = first_stage()

    @pl.when(first)
    def _():
        out_ref[...] = one_ref[...]

    @pl.when(jnp.logical_not(first))
    def _():
        out_ref[...] = two_ref[...]


def first_stage():
    place = lax.axis_index("phase") % 4
    return (place == 1) | (place == 2)


def flipped():
    return lax.axis_index("phase") % 4 == 2


def pack_kernel(qkv, out, chunk_p, chunk_q, chunks):
    first = jnp.where(first_stage(), 0, 2)
    turned = jnp.where(flipped(), 1, 0)
    for which, chunk in enumerate((chunk_p, chunk_q)):
        section = first + jnp.bitwise_xor(turned, which)
        for i in range(3):
            unit = qkv[section, :, i * WIDTH : (i + 1) * WIDTH]
            chunk[i] = unit
            chunks[4 * which + i] = unit
        for half in range(2):
            unit = out[section, :, half * WIDTH : (half + 1) * WIDTH]
            chunk[3, half * 80 : half * 80 + 80] = unit
            chunks[4 * which + 3, half * 80 : half * 80 + 80] = unit


def pack(w_qkv, w_out):
    vmem = pl.BlockSpec(memory_space=pltpu.VMEM)
    return pl.pallas_call(
        pack_kernel,
        out_shape=[jax.ShapeDtypeStruct((n, 160, WIDTH), jnp.bfloat16) for n in (4, 4, 8)],
        in_specs=[vmem] * 2,
        out_specs=[vmem] * 3,
        compiler_params=pltpu.CompilerParams(vmem_limit_bytes=8 * 1024 * 1024),
        cost_estimate=SMALL,
        name="pack",
    )(w_qkv, w_out)


def choose(name, one, two):
    vmem = pl.BlockSpec(memory_space=pltpu.VMEM)
    return pl.pallas_call(
        choose_kernel,
        out_shape=jax.ShapeDtypeStruct(one.shape, one.dtype),
        in_specs=[vmem] * 2,
        out_specs=vmem,
        compiler_params=pltpu.CompilerParams(vmem_limit_bytes=8 * 1024 * 1024),
        cost_estimate=SMALL,
        name=name,
    )(one, two)


def cores(block):
    return lax.ppermute(block, "dp", [(j, j ^ 1) for j in range(lax.axis_size("dp"))])


def plane(block, turn):
    pairs = [(j, j ^ (2 if j % 2 == turn else 4)) for j in range(lax.axis_size("dp"))]
    return lax.ppermute(block, "dp", pairs)


def by_stage(block, one, two):
    planes = lax.axis_size("phase")
    pairs = []
    for j in range(lax.axis_size("dp")):
        for z in range(planes):
            to = (one if z % 4 in (1, 2) else two)(j, z)
            pairs.append((j * planes + z, to[0] * planes + to[1]))
    return lax.ppermute(block, ("dp", "phase"), pairs)


def across(block):
    size = lax.axis_size("phase")
    return lax.ppermute(block, "phase", [(j, j ^ 1) for j in range(size)])


def staged_body(patches, window_ids, norm_gain, w_qkv, w_out, merge_gain):
    tie = lax.optimization_barrier
    gains = norm_gain.reshape(SECTIONS, 1, D_VIS)
    merge = merge_gain.reshape(1, D_VIS)

    chunk_p, chunk_q, chunks = pack(w_qkv, w_out)
    p1, p2 = plane(chunk_p, 0), plane(chunk_p, 1)
    own_other = cores(chunks)
    own_other, late_q, theirs, their_ids = tie((own_other, chunk_q, patches, window_ids))
    q2 = plane(late_q, 1)

    def core(j, z):
        return j ^ 1, z

    q1_two = by_stage(late_q, core, lambda j, z: (j ^ (2 if j % 2 == 0 else 4), z))
    other, other_ids = across(theirs), across(their_ids)
    p1, p2, q2, q1_two, other, other_ids = tie((p1, p2, q2, q1_two, other, other_ids))
    q1 = by_stage(p1, lambda j, z: (j, z ^ 3), core)
    p3, q3 = plane(p1, 1), plane(q2, 0)
    near = [cores(block) for block in (p1, p2, q2, q1_two)]
    q1, p3, q3, near[0], near[1], near[2] = tie((q1, p3, q3, near[0], near[1], near[2]))
    p = (chunk_p, p1, p2, p3, own_other, near[0], near[1], cores(p3))
    q = (chunk_q, q1, q2, q3, own_other, cores(q1), near[2], cores(q3))
    weights = assemble(1, p, q)

    half_own = run_stage(1, patches, window_ids, gains, merge, weights)
    half_own_far = across(half_own)
    half_own, other = tie((half_own, other))
    half_other = run_stage(1, other, other_ids, gains, merge, weights)
    half_other_far = across(half_other)
    q = (chunk_q, q1_two, q2, q3, own_other, near[3], near[2], q[7])
    half_other, *blocks = tie((half_other, *p, *q))
    weights = assemble(2, blocks[:8], blocks[8:], weights)
    result_other = run_stage(2, half_own_far, other_ids, gains, merge, weights)
    back = across(result_other)
    half_other_far, result_other = tie((half_other_far, result_other))
    result_own = run_stage(2, half_other_far, window_ids, gains, merge, weights)
    return choose("result", back, result_own)


def plain_section(acts, marks, gain, weight_qkv, weight_out):
    rows = acts.shape[0]
    values_f = acts.astype(jnp.float32)
    normed = normed_rows(values_f, gain).astype(jnp.bfloat16)
    qkv = jnp.dot(normed, weight_qkv, preferred_element_type=jnp.float32).astype(jnp.bfloat16)
    query, keys, vals = (
        qkv[:, i * WIDTH : (i + 1) * WIDTH].reshape(rows, HEADS, HEAD_DIM) for i in range(3)
    )
    scores = jnp.einsum(
        "qhd,khd->hqk", query, keys, preferred_element_type=jnp.float32
    ) * HEAD_DIM ** (-0.5)
    same = marks[:, None] == marks[None, :]
    scores = jnp.where(same[None], scores, jnp.float32(NEG))
    probs = jax.nn.softmax(scores, axis=-1).astype(jnp.bfloat16)
    context = jnp.einsum("hqk,khd->qhd", probs, vals, preferred_element_type=jnp.float32)
    context = context.astype(jnp.bfloat16).reshape(rows, WIDTH)
    update = jnp.dot(context, weight_out, preferred_element_type=jnp.float32)
    return (values_f + update).astype(jnp.bfloat16)


def plain_body(patches, window_ids, norm_gain, w_qkv, w_out, merge_gain):
    acts = patches
    for k in range(w_qkv.shape[0]):
        local_qkv, local_out, acts = lax.optimization_barrier((w_qkv[k], w_out[k], acts))
        weight_qkv = lax.all_gather(local_qkv, "dp", axis=0, tiled=True)
        weight_out = lax.all_gather(local_out, "dp", axis=0, tiled=True)
        acts = plain_section(acts, window_ids[0], norm_gain[k], weight_qkv, weight_out)
    final = normed_rows(acts.astype(jnp.float32), merge_gain).astype(jnp.bfloat16)
    return final.reshape(-1, 4 * D_VIS)


def body(patches, window_ids, norm_gain, w_qkv, w_out, merge_gain):
    staged = lax.axis_size("dp") == 8 and lax.axis_size("phase") % 4 == 0
    run = staged_body if staged else plain_body
    return run(patches, window_ids, norm_gain, w_qkv, w_out, merge_gain)


def solution(mesh):
    in_specs = (
        P(("dp", "phase"), None),
        P(("dp", "phase"), None),
        P(),
        P(None, "dp", None),
        P(None, "dp", None),
        P(),
    )
    out_specs = P(("dp", "phase"), None)
    return jax.shard_map(body, mesh=mesh, in_specs=in_specs, out_specs=out_specs, check_vma=False)
```

```python
import functools

import jax
import jax.numpy as jnp
from jax import lax
from jax.experimental import pallas as pl
from jax.experimental.pallas import tpu as pltpu
from jax.sharding import PartitionSpec as P

D_VIS = 1280
HEADS = 8
HEAD_DIM = 80
WIDTH = HEADS * HEAD_DIM
SECTIONS = 4
LANES = 128
EPS = 1e-06
NEG = -1e30
SMALL = pl.CostEstimate(flops=1, bytes_accessed=1, transcendentals=1)


def normed_rows(values, gain):
    scale = lax.rsqrt(jnp.mean(values * values, axis=-1, keepdims=True) + EPS)
    return values * scale * gain


def attend(qkv, row_ids):
    query, keys, vals = qkv
    rows = query.shape[0]
    across = jnp.broadcast_to(row_ids, (rows, rows))
    same = across == across.T
    lane = lax.broadcasted_iota(jnp.int32, (rows, LANES), 1)
    tiles = [None] * (WIDTH // LANES)
    for head in range(HEADS):
        first, last = head * HEAD_DIM, (head + 1) * HEAD_DIM
        low, high = first // LANES, -(-last // LANES)
        span = slice(low * LANES, high * LANES)
        inside = []
        for tile in range(low, high):
            place = lane + tile * LANES
            inside.append((place >= first) & (place < last))
        part = jnp.concatenate(
            [
                jnp.where(mask, query[:, (low + i) * LANES : (low + i + 1) * LANES], 0)
                for i, mask in enumerate(inside)
            ],
            axis=1,
        )
        scores = lax.dot_general(
            part, keys[:, span], (((1,), (1,)), ((), ())), preferred_element_type=jnp.float32
        )
        scores = jnp.where(same, scores * HEAD_DIM ** (-0.5), NEG)
        weights = jnp.exp(scores - jnp.max(scores, axis=-1, keepdims=True))
        probs = weights * (1.0 / jnp.sum(weights, axis=-1, keepdims=True))
        mixed = jnp.dot(
            probs.astype(jnp.bfloat16), vals[:, span], preferred_element_type=jnp.float32
        )
        for i, mask in enumerate(inside):
            kept = jnp.where(mask, mixed[:, i * LANES : (i + 1) * LANES], 0.0)
            tile = low + i
            tiles[tile] = kept if tiles[tile] is None else tiles[tile] + kept
    return jnp.concatenate(tiles, axis=1).astype(jnp.bfloat16)


def stage_kernel(stage, *refs):
    pl.when(first_stage() == (stage == 1))(functools.partial(two_sections, stage, *refs))


def two_sections(stage, acts_ref, ids_ref, gain_ref, merge_ref, one_ref, two_ref, out_ref, flow, sheets):
    rows = flow.shape[0]
    flow[...] = acts_ref[...].astype(jnp.float32)
    for i, held in enumerate((one_ref, two_ref)):
        normed = normed_rows(flow[...], gain_ref[2 * stage - 2 + i]).astype(jnp.bfloat16)
        qkv = [
            jnp.dot(normed, held[j], preferred_element_type=jnp.float32).astype(jnp.bfloat16)
            for j in range(3)
        ]
        context = attend(qkv, ids_ref[...])
        for half in range(2):
            at = slice(half * WIDTH, (half + 1) * WIDTH)
            moved = jnp.dot(context, held[3, at], preferred_element_type=jnp.float32)
            flow[:, at] = (flow[:, at] + moved).astype(jnp.bfloat16).astype(jnp.float32)
    if stage == 1:
        out_ref[...] = flow[...].astype(jnp.bfloat16)
    else:
        final = normed_rows(flow[...], merge_ref[...])
        for tile in range(D_VIS // LANES):
            sheets[tile] = final[:, tile * LANES : (tile + 1) * LANES]
        for i in range(4):
            for tile in range(D_VIS // LANES):
                at = i * D_VIS + tile * LANES
                out_ref[:, at : at + LANES] = sheets[
                    tile, pl.ds(i, rows // 4, stride=4), :
                ].astype(jnp.bfloat16)


def run_stage(stage, acts, ids, gains, merge, weights):
    rows = acts.shape[0]
    vmem = pl.BlockSpec(memory_space=pltpu.VMEM)
    args = [acts, ids, gains, merge] + list(weights)
    return pl.pallas_call(
        functools.partial(stage_kernel, stage),
        out_shape=jax.ShapeDtypeStruct(
            (rows, D_VIS) if stage == 1 else (rows // 4, 4 * D_VIS), jnp.bfloat16
        ),
        in_specs=[vmem] * len(args),
        out_specs=vmem,
        scratch_shapes=[
            pltpu.VMEM((rows, D_VIS), jnp.float32),
            pltpu.VMEM((D_VIS // LANES, rows, LANES), jnp.float32),
        ],
        compiler_params=pltpu.CompilerParams(vmem_limit_bytes=8 * 1024 * 1024),
        cost_estimate=SMALL,
        name=f"stage_{stage}",
    )(*args)


def assemble_kernel(stage, n_given, *refs):
    blocks, whole = refs[n_given : n_given + 16], refs[n_given + 16 :]
    turned, early = flipped(), first_stage()
    if stage == 2:
        pl.when(jnp.logical_not(early))(functools.partial(put_in_order, blocks, whole))
    else:
        for swapped in (False, True):
            pl.when(early & (turned == swapped))(
                functools.partial(put_in_order, blocks, whole[::-1] if swapped else whole)
            )


def put_in_order(blocks, whole):
    me = lax.axis_index("dp")
    one = jnp.where(me % 2 == 0, 2, 4)
    for which in range(2):
        for i, distance in enumerate((0, one, 6 - one, 6, 1, 7 - one, 1 + one, 7)):
            block = blocks[8 * which + i]
            first = 4 * which if block.shape[0] == 8 else 0
            owner = jnp.bitwise_xor(me, distance)
            for unit in range(3):
                where = pl.ds(pl.multiple_of(owner * 160, 16), 160)
                whole[which][unit, where] = block[first + unit]
            for half in range(2):
                where = pl.ds(pl.multiple_of(owner * 80 + half * WIDTH, 16), 80)
                whole[which][3, where] = block[first + 3, half * 80 : half * 80 + 80]


def assemble(stage, p, q, given=()):
    vmem = pl.BlockSpec(memory_space=pltpu.VMEM)
    return pl.pallas_call(
        functools.partial(assemble_kernel, stage, len(given)),
        out_shape=[jax.ShapeDtypeStruct((4, D_VIS, WIDTH), jnp.bfloat16)] * 2,
        in_specs=[vmem] * (len(given) + 16),
        out_specs=[vmem] * 2,
        input_output_aliases={i: i for i in range(len(given))},
        compiler_params=pltpu.CompilerParams(vmem_limit_bytes=8 * 1024 * 1024),
        cost_estimate=SMALL,
        name="assemble",
    )(*given, *p, *q)


def choose_kernel(one_ref, two_ref, out_ref):
    first = first_stage()

    @pl.when(first)
    def _():
        out_ref[...] = one_ref[...]

    @pl.when(jnp.logical_not(first))
    def _():
        out_ref[...] = two_ref[...]


def first_stage():
    place = lax.axis_index("phase") % 4
    return (place == 1) | (place == 2)


def flipped():
    return lax.axis_index("phase") % 4 == 2


def pack_kernel(qkv, out, chunk_p, chunk_q, chunks):
    first = jnp.where(first_stage(), 0, 2)
    turned = jnp.where(flipped(), 1, 0)
    for which, chunk in enumerate((chunk_p, chunk_q)):
        section = first + jnp.bitwise_xor(turned, which)
        for i in range(3):
            unit = qkv[section, :, i * WIDTH : (i + 1) * WIDTH]
            chunk[i] = unit
            chunks[4 * which + i] = unit
        for half in range(2):
            unit = out[section, :, half * WIDTH : (half + 1) * WIDTH]
            chunk[3, half * 80 : half * 80 + 80] = unit
            chunks[4 * which + 3, half * 80 : half * 80 + 80] = unit


def pack(w_qkv, w_out):
    vmem = pl.BlockSpec(memory_space=pltpu.VMEM)
    return pl.pallas_call(
        pack_kernel,
        out_shape=[jax.ShapeDtypeStruct((n, 160, WIDTH), jnp.bfloat16) for n in (4, 4, 8)],
        in_specs=[vmem] * 2,
        out_specs=[vmem] * 3,
        compiler_params=pltpu.CompilerParams(vmem_limit_bytes=8 * 1024 * 1024),
        cost_estimate=SMALL,
        name="pack",
    )(w_qkv, w_out)


def choose(name, one, two):
    vmem = pl.BlockSpec(memory_space=pltpu.VMEM)
    return pl.pallas_call(
        choose_kernel,
        out_shape=jax.ShapeDtypeStruct(one.shape, one.dtype),
        in_specs=[vmem] * 2,
        out_specs=vmem,
        compiler_params=pltpu.CompilerParams(vmem_limit_bytes=8 * 1024 * 1024),
        cost_estimate=SMALL,
        name=name,
    )(one, two)


def cores(block):
    return lax.ppermute(block, "dp", [(j, j ^ 1) for j in range(lax.axis_size("dp"))])


def plane(block, turn):
    pairs = [(j, j ^ (2 if j % 2 == turn else 4)) for j in range(lax.axis_size("dp"))]
    return lax.ppermute(block, "dp", pairs)


def by_stage(block, one, two):
    planes = lax.axis_size("phase")
    pairs = []
    for j in range(lax.axis_size("dp")):
        for z in range(planes):
            to = (one if z % 4 in (1, 2) else two)(j, z)
            pairs.append((j * planes + z, to[0] * planes + to[1]))
    return lax.ppermute(block, ("dp", "phase"), pairs)


def across(block):
    size = lax.axis_size("phase")
    return lax.ppermute(block, "phase", [(j, j ^ 1) for j in range(size)])


def staged_body(patches, window_ids, norm_gain, w_qkv, w_out, merge_gain):
    tie = lax.optimization_barrier
    gains = norm_gain.reshape(SECTIONS, 1, D_VIS)
    merge = merge_gain.reshape(1, D_VIS)

    chunk_p, chunk_q, chunks = pack(w_qkv, w_out)
    p1, p2 = plane(chunk_p, 0), plane(chunk_p, 1)
    own_other = cores(chunks)
    own_other, late_q, theirs, their_ids = tie((own_other, chunk_q, patches, window_ids))
    q2 = plane(late_q, 1)

    def core(j, z):
        return j ^ 1, z

    q1_two = by_stage(late_q, core, lambda j, z: (j ^ (2 if j % 2 == 0 else 4), z))
    other, other_ids = across(theirs), across(their_ids)
    p1, p2, q2, q1_two, other, other_ids = tie((p1, p2, q2, q1_two, other, other_ids))
    q1 = by_stage(p1, lambda j, z: (j, z ^ 3), core)
    p3, q3 = plane(p1, 1), plane(q2, 0)
    near = [cores(block) for block in (p1, p2, q2, q1_two)]
    p3, q3, near[0], near[1] = tie((p3, q3, near[0], near[1]))
    q1, near[2] = tie((q1, near[2]))
    p = (chunk_p, p1, p2, p3, own_other, near[0], near[1], cores(p3))
    q = (chunk_q, q1, q2, q3, own_other, cores(q1), near[2], cores(q3))
    weights = assemble(1, p, q)

    half_own = run_stage(1, patches, window_ids, gains, merge, weights)
    half_own_far = across(half_own)
    half_own, other = tie((half_own, other))
    half_other = run_stage(1, other, other_ids, gains, merge, weights)
    half_other_far = across(half_other)
    q = (chunk_q, q1_two, q2, q3, own_other, near[3], near[2], q[7])
    half_other, *blocks = tie((half_other, *p, *q))
    weights = assemble(2, blocks[:8], blocks[8:], weights)
    result_other = run_stage(2, half_own_far, other_ids, gains, merge, weights)
    back = across(result_other)
    half_other_far, result_other = tie((half_other_far, result_other))
    result_own = run_stage(2, half_other_far, window_ids, gains, merge, weights)
    return choose("result", back, result_own)


def plain_section(acts, marks, gain, weight_qkv, weight_out):
    rows = acts.shape[0]
    values_f = acts.astype(jnp.float32)
    normed = normed_rows(values_f, gain).astype(jnp.bfloat16)
    qkv = jnp.dot(normed, weight_qkv, preferred_element_type=jnp.float32).astype(jnp.bfloat16)
    query, keys, vals = (
        qkv[:, i * WIDTH : (i + 1) * WIDTH].reshape(rows, HEADS, HEAD_DIM) for i in range(3)
    )
    scores = jnp.einsum(
        "qhd,khd->hqk", query, keys, preferred_element_type=jnp.float32
    ) * HEAD_DIM ** (-0.5)
    same = marks[:, None] == marks[None, :]
    scores = jnp.where(same[None], scores, jnp.float32(NEG))
    probs = jax.nn.softmax(scores, axis=-1).astype(jnp.bfloat16)
    context = jnp.einsum("hqk,khd->qhd", probs, vals, preferred_element_type=jnp.float32)
    context = context.astype(jnp.bfloat16).reshape(rows, WIDTH)
    update = jnp.dot(context, weight_out, preferred_element_type=jnp.float32)
    return (values_f + update).astype(jnp.bfloat16)


def plain_body(patches, window_ids, norm_gain, w_qkv, w_out, merge_gain):
    acts = patches
    for k in range(w_qkv.shape[0]):
        local_qkv, local_out, acts = lax.optimization_barrier((w_qkv[k], w_out[k], acts))
        weight_qkv = lax.all_gather(local_qkv, "dp", axis=0, tiled=True)
        weight_out = lax.all_gather(local_out, "dp", axis=0, tiled=True)
        acts = plain_section(acts, window_ids[0], norm_gain[k], weight_qkv, weight_out)
    final = normed_rows(acts.astype(jnp.float32), merge_gain).astype(jnp.bfloat16)
    return final.reshape(-1, 4 * D_VIS)


def body(patches, window_ids, norm_gain, w_qkv, w_out, merge_gain):
    staged = lax.axis_size("dp") == 8 and lax.axis_size("phase") % 4 == 0
    run = staged_body if staged else plain_body
    return run(patches, window_ids, norm_gain, w_qkv, w_out, merge_gain)


def solution(mesh):
    in_specs = (
        P(("dp", "phase"), None),
        P(("dp", "phase"), None),
        P(),
        P(None, "dp", None),
        P(None, "dp", None),
        P(),
    )
    out_specs = P(("dp", "phase"), None)
    return jax.shard_map(body, mesh=mesh, in_specs=in_specs, out_specs=out_specs, check_vma=False)
```

```python
import functools

import jax
import jax.numpy as jnp
from jax import lax
from jax.experimental import pallas as pl
from jax.experimental.pallas import tpu as pltpu
from jax.sharding import PartitionSpec as P

D_VIS = 1280
HEADS = 8
HEAD_DIM = 80
WIDTH = HEADS * HEAD_DIM
SECTIONS = 4
LANES = 128
EPS = 1e-06
NEG = -1e30
SMALL = pl.CostEstimate(flops=1, bytes_accessed=1, transcendentals=1)


def normed_rows(values, gain):
    scale = lax.rsqrt(jnp.mean(values * values, axis=-1, keepdims=True) + EPS)
    return values * scale * gain


def attend(qkv, row_ids):
    query, keys, vals = qkv
    rows = query.shape[0]
    across = jnp.broadcast_to(row_ids, (rows, rows))
    same = across == across.T
    lane = lax.broadcasted_iota(jnp.int32, (rows, LANES), 1)
    tiles = [None] * (WIDTH // LANES)
    for head in range(HEADS):
        first, last = head * HEAD_DIM, (head + 1) * HEAD_DIM
        low, high = first // LANES, -(-last // LANES)
        span = slice(low * LANES, high * LANES)
        inside = []
        for tile in range(low, high):
            place = lane + tile * LANES
            inside.append((place >= first) & (place < last))
        part = jnp.concatenate(
            [
                jnp.where(mask, query[:, (low + i) * LANES : (low + i + 1) * LANES], 0)
                for i, mask in enumerate(inside)
            ],
            axis=1,
        )
        scores = lax.dot_general(
            part, keys[:, span], (((1,), (1,)), ((), ())), preferred_element_type=jnp.float32
        )
        scores = jnp.where(same, scores * HEAD_DIM ** (-0.5), NEG)
        weights = jnp.exp(scores - jnp.max(scores, axis=-1, keepdims=True))
        probs = weights * (1.0 / jnp.sum(weights, axis=-1, keepdims=True))
        mixed = jnp.dot(
            probs.astype(jnp.bfloat16), vals[:, span], preferred_element_type=jnp.float32
        )
        for i, mask in enumerate(inside):
            kept = jnp.where(mask, mixed[:, i * LANES : (i + 1) * LANES], 0.0)
            tile = low + i
            tiles[tile] = kept if tiles[tile] is None else tiles[tile] + kept
    return jnp.concatenate(tiles, axis=1).astype(jnp.bfloat16)


def stage_kernel(stage, *refs):
    pl.when(first_stage() == (stage == 1))(functools.partial(two_sections, stage, *refs))


def two_sections(stage, acts_ref, ids_ref, gain_ref, merge_ref, one_ref, two_ref, out_ref, flow, sheets):
    rows = flow.shape[0]
    flow[...] = acts_ref[...].astype(jnp.float32)
    for i, held in enumerate((one_ref, two_ref)):
        normed = normed_rows(
            flow[...], gain_ref[2 * stage - 2 + i : 2 * stage - 1 + i]
        ).astype(jnp.bfloat16)
        qkv = [
            jnp.dot(normed, held[j], preferred_element_type=jnp.float32).astype(jnp.bfloat16)
            for j in range(3)
        ]
        context = attend(qkv, ids_ref[...])
        for half in range(2):
            at = slice(half * WIDTH, (half + 1) * WIDTH)
            moved = jnp.dot(context, held[3, at], preferred_element_type=jnp.float32)
            flow[:, at] = (flow[:, at] + moved).astype(jnp.bfloat16).astype(jnp.float32)
    if stage == 1:
        out_ref[...] = flow[...].astype(jnp.bfloat16)
    else:
        final = normed_rows(flow[...], merge_ref[...])
        for tile in range(D_VIS // LANES):
            sheets[tile] = final[:, tile * LANES : (tile + 1) * LANES]
        for i in range(4):
            for tile in range(D_VIS // LANES):
                at = i * D_VIS + tile * LANES
                out_ref[:, at : at + LANES] = sheets[
                    tile, pl.ds(i, rows // 4, stride=4), :
                ].astype(jnp.bfloat16)


def run_stage(stage, acts, ids, gains, merge, weights):
    rows = acts.shape[0]
    vmem = pl.BlockSpec(memory_space=pltpu.VMEM)
    args = [acts, ids, gains, merge] + list(weights)
    return pl.pallas_call(
        functools.partial(stage_kernel, stage),
        out_shape=jax.ShapeDtypeStruct(
            (rows, D_VIS) if stage == 1 else (rows // 4, 4 * D_VIS), jnp.bfloat16
        ),
        in_specs=[vmem] * len(args),
        out_specs=vmem,
        scratch_shapes=[
            pltpu.VMEM((rows, D_VIS), jnp.float32),
            pltpu.VMEM((D_VIS // LANES, rows, LANES), jnp.float32),
        ],
        compiler_params=pltpu.CompilerParams(vmem_limit_bytes=8 * 1024 * 1024),
        cost_estimate=SMALL,
        name=f"stage_{stage}",
    )(*args)


def assemble_kernel(stage, n_given, *refs):
    blocks, whole = refs[n_given : n_given + 16], refs[n_given + 16 :]
    turned, early = flipped(), first_stage()
    if stage == 2:
        pl.when(jnp.logical_not(early))(functools.partial(put_in_order, blocks, whole))
    else:
        for swapped in (False, True):
            pl.when(early & (turned == swapped))(
                functools.partial(put_in_order, blocks, whole[::-1] if swapped else whole)
            )


def put_in_order(blocks, whole):
    me = lax.axis_index("dp")
    one = jnp.where(me % 2 == 0, 2, 4)
    for which in range(2):
        for i, distance in enumerate((0, one, 6 - one, 6, 1, 7 - one, 1 + one, 7)):
            block = blocks[8 * which + i]
            first = 4 * which if block.shape[0] == 8 else 0
            owner = jnp.bitwise_xor(me, distance)
            for unit in range(3):
                where = pl.ds(pl.multiple_of(owner * 160, 16), 160)
                whole[which][unit, where] = block[first + unit]
            for half in range(2):
                where = pl.ds(pl.multiple_of(owner * 80 + half * WIDTH, 16), 80)
                whole[which][3, where] = block[first + 3, half * 80 : half * 80 + 80]


def assemble(stage, p, q, given=()):
    vmem = pl.BlockSpec(memory_space=pltpu.VMEM)
    return pl.pallas_call(
        functools.partial(assemble_kernel, stage, len(given)),
        out_shape=[jax.ShapeDtypeStruct((4, D_VIS, WIDTH), jnp.bfloat16)] * 2,
        in_specs=[vmem] * (len(given) + 16),
        out_specs=[vmem] * 2,
        input_output_aliases={i: i for i in range(len(given))},
        compiler_params=pltpu.CompilerParams(vmem_limit_bytes=8 * 1024 * 1024),
        cost_estimate=SMALL,
        name="assemble",
    )(*given, *p, *q)


def choose_kernel(one_ref, two_ref, out_ref):
    first = first_stage()

    @pl.when(first)
    def _():
        out_ref[...] = one_ref[...]

    @pl.when(jnp.logical_not(first))
    def _():
        out_ref[...] = two_ref[...]


def first_stage():
    place = lax.axis_index("phase") % 4
    return (place == 1) | (place == 2)


def flipped():
    return lax.axis_index("phase") % 4 == 2


def pack_kernel(qkv, out, chunk_p, chunk_q, chunks):
    first = jnp.where(first_stage(), 0, 2)
    turned = jnp.where(flipped(), 1, 0)
    for which, chunk in enumerate((chunk_p, chunk_q)):
        section = first + jnp.bitwise_xor(turned, which)
        for i in range(3):
            unit = qkv[section, :, i * WIDTH : (i + 1) * WIDTH]
            chunk[i] = unit
            chunks[4 * which + i] = unit
        for half in range(2):
            unit = out[section, :, half * WIDTH : (half + 1) * WIDTH]
            chunk[3, half * 80 : half * 80 + 80] = unit
            chunks[4 * which + 3, half * 80 : half * 80 + 80] = unit


def pack(w_qkv, w_out):
    vmem = pl.BlockSpec(memory_space=pltpu.VMEM)
    return pl.pallas_call(
        pack_kernel,
        out_shape=[jax.ShapeDtypeStruct((n, 160, WIDTH), jnp.bfloat16) for n in (4, 4, 8)],
        in_specs=[vmem] * 2,
        out_specs=[vmem] * 3,
        compiler_params=pltpu.CompilerParams(vmem_limit_bytes=8 * 1024 * 1024),
        cost_estimate=SMALL,
        name="pack",
    )(w_qkv, w_out)


def choose(name, one, two):
    vmem = pl.BlockSpec(memory_space=pltpu.VMEM)
    return pl.pallas_call(
        choose_kernel,
        out_shape=jax.ShapeDtypeStruct(one.shape, one.dtype),
        in_specs=[vmem] * 2,
        out_specs=vmem,
        compiler_params=pltpu.CompilerParams(vmem_limit_bytes=8 * 1024 * 1024),
        cost_estimate=SMALL,
        name=name,
    )(one, two)


def cores(block):
    return lax.ppermute(block, "dp", [(j, j ^ 1) for j in range(lax.axis_size("dp"))])


def plane(block, turn):
    pairs = [(j, j ^ (2 if j % 2 == turn else 4)) for j in range(lax.axis_size("dp"))]
    return lax.ppermute(block, "dp", pairs)


def by_stage(block, one, two):
    planes = lax.axis_size("phase")
    pairs = []
    for j in range(lax.axis_size("dp")):
        for z in range(planes):
            to = (one if z % 4 in (1, 2) else two)(j, z)
            pairs.append((j * planes + z, to[0] * planes + to[1]))
    return lax.ppermute(block, ("dp", "phase"), pairs)


def across(block):
    size = lax.axis_size("phase")
    return lax.ppermute(block, "phase", [(j, j ^ 1) for j in range(size)])


def staged_body(patches, window_ids, norm_gain, w_qkv, w_out, merge_gain):
    tie = lax.optimization_barrier
    gains = norm_gain
    merge = merge_gain.reshape(1, D_VIS)

    chunk_p, chunk_q, chunks = pack(w_qkv, w_out)
    p1, p2 = plane(chunk_p, 0), plane(chunk_p, 1)
    own_other = cores(chunks)
    own_other, late_q, theirs, their_ids = tie((own_other, chunk_q, patches, window_ids))
    q2 = plane(late_q, 1)

    def core(j, z):
        return j ^ 1, z

    q1_two = by_stage(late_q, core, lambda j, z: (j ^ (2 if j % 2 == 0 else 4), z))
    other, other_ids = across(theirs), across(their_ids)
    p1, p2, q2, q1_two, other, other_ids = tie((p1, p2, q2, q1_two, other, other_ids))
    q1 = by_stage(p1, lambda j, z: (j, z ^ 3), core)
    p3, q3 = plane(p1, 1), plane(q2, 0)
    near = [cores(block) for block in (p1, p2, q2, q1_two)]
    p3, q3, near[0], near[1] = tie((p3, q3, near[0], near[1]))
    q1, near[2] = tie((q1, near[2]))
    p = (chunk_p, p1, p2, p3, own_other, near[0], near[1], cores(p3))
    q = (chunk_q, q1, q2, q3, own_other, cores(q1), near[2], cores(q3))
    weights = assemble(1, p, q)

    half_own = run_stage(1, patches, window_ids, gains, merge, weights)
    half_own_far = across(half_own)
    half_own, other = tie((half_own, other))
    half_other = run_stage(1, other, other_ids, gains, merge, weights)
    half_other_far = across(half_other)
    q = (chunk_q, q1_two, q2, q3, own_other, near[3], near[2], q[7])
    half_other, *blocks = tie((half_other, *p, *q))
    weights = assemble(2, blocks[:8], blocks[8:], weights)
    result_other = run_stage(2, half_own_far, other_ids, gains, merge, weights)
    back = across(result_other)
    half_other_far, result_other = tie((half_other_far, result_other))
    result_own = run_stage(2, half_other_far, window_ids, gains, merge, weights)
    return choose("result", back, result_own)


def plain_section(acts, marks, gain, weight_qkv, weight_out):
    rows = acts.shape[0]
    values_f = acts.astype(jnp.float32)
    normed = normed_rows(values_f, gain).astype(jnp.bfloat16)
    qkv = jnp.dot(normed, weight_qkv, preferred_element_type=jnp.float32).astype(jnp.bfloat16)
    query, keys, vals = (
        qkv[:, i * WIDTH : (i + 1) * WIDTH].reshape(rows, HEADS, HEAD_DIM) for i in range(3)
    )
    scores = jnp.einsum(
        "qhd,khd->hqk", query, keys, preferred_element_type=jnp.float32
    ) * HEAD_DIM ** (-0.5)
    same = marks[:, None] == marks[None, :]
    scores = jnp.where(same[None], scores, jnp.float32(NEG))
    probs = jax.nn.softmax(scores, axis=-1).astype(jnp.bfloat16)
    context = jnp.einsum("hqk,khd->qhd", probs, vals, preferred_element_type=jnp.float32)
    context = context.astype(jnp.bfloat16).reshape(rows, WIDTH)
    update = jnp.dot(context, weight_out, preferred_element_type=jnp.float32)
    return (values_f + update).astype(jnp.bfloat16)


def plain_body(patches, window_ids, norm_gain, w_qkv, w_out, merge_gain):
    acts = patches
    for k in range(w_qkv.shape[0]):
        local_qkv, local_out, acts = lax.optimization_barrier((w_qkv[k], w_out[k], acts))
        weight_qkv = lax.all_gather(local_qkv, "dp", axis=0, tiled=True)
        weight_out = lax.all_gather(local_out, "dp", axis=0, tiled=True)
        acts = plain_section(acts, window_ids[0], norm_gain[k], weight_qkv, weight_out)
    final = normed_rows(acts.astype(jnp.float32), merge_gain).astype(jnp.bfloat16)
    return final.reshape(-1, 4 * D_VIS)


def body(patches, window_ids, norm_gain, w_qkv, w_out, merge_gain):
    staged = lax.axis_size("dp") == 8 and lax.axis_size("phase") % 4 == 0
    run = staged_body if staged else plain_body
    return run(patches, window_ids, norm_gain, w_qkv, w_out, merge_gain)


def solution(mesh):
    in_specs = (
        P(("dp", "phase"), None),
        P(("dp", "phase"), None),
        P(),
        P(None, "dp", None),
        P(None, "dp", None),
        P(),
    )
    out_specs = P(("dp", "phase"), None)
    return jax.shard_map(body, mesh=mesh, in_specs=in_specs, out_specs=out_specs, check_vma=False)
```
